128 devices in a mesh: ctx: 8 (over y_lo, x), head: 16 (over z, y_hi, core).
Axes of the slice: x: 4, y: 4 (y_hi: 2, y_lo: 2; y = y_hi * 2 + y_lo), z: 4, core: 2. Of those that a mesh axis runs over, the one named last changes fastest.
Arguments:
- latent: bfloat16 [2048, 576], P('ctx'), may hold values from -6 to 6
- queries: bfloat16 [2048, 24576], P('ctx', 'head'), may hold values from -300 to 300
- up_weight: bfloat16 [512, 32768], P(None, 'head'), may hold values from -0.25 to 0.25
- out_grad: bfloat16 [2048, 16384], P('ctx', 'head'), may hold values from -6 to 6
- logratio: float32 [2048], P('ctx'), may hold values from -1.5 to 1.5
- student_logprob: float32 [2048], P('ctx'), may hold values from -4 to -0.05
- teacher_logprob: float32 [2048], P('ctx'), may hold values from -4 to -0.05
- group_order: int32 [16], replicated, may hold values from 0 to 15, each once
Outputs:
- attn_output: bfloat16 [2048, 16384], P('ctx', 'head')
- query_grad: bfloat16 [2048, 24576], P('ctx', 'head')
- latent_grad: float32 [2048, 576], P(('ctx', 'head'))
- weight_grad: float32 [512, 32768], P('ctx', 'head')
The draws below stay inside these ranges and needn't reach their ends.
Inputs may be any that keep to these rules, and one draw needn't show every extreme that they name: Row r of the sequence arrays stands at position group_order[r // 128] * 128 + r % 128 of the rollout.
All inputs are finite; a program needn't handle non-finite values.
Results may differ from the reference program's by a relative error of at most 0.035.
Values may be sent and summed in bfloat16 or wider, within the bound.
No kernel may reach another device: no remote copies, remote signals or barrier semaphores. Data moves between devices by JAX's collectives and lax.ppermute only.
A program may use at most 64 MiB of HBM per device.

```python
import jax
import jax.numpy as jnp
from jax import lax

H = 128
NOPE = 128
VDIM = 128
KV_RANK = 512
TOK_DEV = 256
LATENT = 576
QK = 192
SEQ = 2048
GROUP = 128
GROUPS = 16
N_CTX = 8


def latent_base(key):
    return jnp.clip(jax.random.normal(key, (SEQ, LATENT), jnp.float32), -6.0, 6.0)


def draw_latent(key, part):
    base = latent_base(key)
    return base.astype(jnp.bfloat16)


def draw_queries(key, part):
    key = jax.random.fold_in(key, 7)
    value_matrix = jnp.clip(jax.random.normal(key, (SEQ, H, QK), jnp.float32), -6.0, 6.0)
    value_matrix = jnp.clip(value_matrix, -300.0, 300.0)
    return value_matrix.reshape(SEQ, H * QK).astype(jnp.bfloat16)


def block_levels(rng, dims, cuts, smallest, top_value):
    factor_of = 1.0
    for position, blocks in cuts:
        draws = jax.random.uniform(jax.random.fold_in(jax.random.fold_in(rng, 6), position), (blocks,), jnp.float32, smallest / len(cuts), top_value / len(cuts))
        factor_of = factor_of * jnp.repeat(jnp.exp(draws), dims[position] // blocks).reshape((-1,) + (1,) * (len(dims) - 1 - position))
    return factor_of


def gaussian(stream_key, shape, scale, reach, split=(), held_as=jnp.bfloat16):
    result = jax.random.normal(stream_key, shape, jnp.float32) * scale
    if len(split) > 0:
        result = block_levels(stream_key, shape, split, -0.22, 0.18) * result
    return jnp.clip(result, min=-reach, max=reach).astype(held_as)


def setup_inputs(seed: int = 0) -> dict:
    keys = jax.random.split(jax.random.key(seed), 9)
    latent = draw_latent(jax.random.fold_in(keys[8], 71), 0)
    queries = draw_queries(jax.random.fold_in(keys[8], 71), 0)
    up_weight = gaussian(keys[2], (KV_RANK, H * (NOPE + VDIM)), KV_RANK ** -0.5, 0.25, ((1, 16),))
    out_grad = gaussian(keys[3], (SEQ, H * VDIM), 1.0, 6.0, ((0, 8), (1, 16)))
    logratio = gaussian(keys[4], (SEQ,), 0.3, 1.5, ((0, 8),), jnp.float32)
    student_logprob = jnp.clip(-4.0 + 3.95 * jax.random.uniform(keys[5], (SEQ,), jnp.float32) ** block_levels(keys[5], (SEQ,), ((0, 8),), -0.2, 0.2), -4.0, -0.05)
    teacher_logprob = jnp.clip(-4.0 + 3.95 * jax.random.uniform(keys[6], (SEQ,), jnp.float32) ** block_levels(keys[6], (SEQ,), ((0, 8),), -0.2, 0.2), -4.0, -0.05)
    group_order = jax.random.permutation(keys[7], GROUPS).astype(jnp.int32)
    return dict(latent=latent, queries=queries, up_weight=up_weight, out_grad=out_grad, logratio=logratio, student_logprob=student_logprob, teacher_logprob=teacher_logprob, group_order=group_order)


def positions_of(group_order, row_count, group_len):
    row_index = jnp.arange(row_count, dtype=jnp.int32)
    group_slot = row_index // group_len
    onehot = group_slot[:, None] == jnp.arange(group_order.shape[0], dtype=jnp.int32)[None, :]
    starts = jnp.sum(jnp.where(onehot, group_order[None, :], 0), axis=1).astype(jnp.int32)
    return starts * group_len + row_index % group_len


def token_weight(logratio, student_logprob, teacher_logprob):
    return jnp.clip(jnp.exp(logratio), 0.8, 1.25) * (teacher_logprob - student_logprob)


def head_block(head_query, head_grad, head_weight, latent, visible, tok_weight):
    logit_scale = QK ** -0.5
    latent_main = latent[:, :KV_RANK]
    key_value = jnp.dot(latent_main, head_weight, preferred_element_type=jnp.float32).astype(jnp.bfloat16)
    key_matrix = jnp.concatenate([key_value[:, :NOPE], latent[:, KV_RANK:]], axis=1).astype(jnp.float32)
    value_matrix = key_value[:, NOPE:].astype(jnp.float32)
    complete_query = head_query.astype(jnp.float32)
    score_matrix = jnp.einsum("jse,ne->jsn", complete_query, key_matrix) * logit_scale
    score_matrix = jnp.where(visible, score_matrix, -jnp.inf)
    row_max = jnp.max(score_matrix, axis=-1, keepdims=True)
    numerator = jnp.exp(score_matrix - row_max)
    attn_prob = numerator / jnp.sum(numerator, axis=-1, keepdims=True)
    probability_lowered = attn_prob.astype(jnp.bfloat16).astype(jnp.float32)
    attention_result = jnp.einsum("gfl,lh->gfh", probability_lowered, value_matrix)
    output_gradient = (tok_weight[..., None] * head_grad.astype(jnp.float32)).astype(jnp.bfloat16).astype(jnp.float32)
    probability_gradient = jnp.einsum("jse,ne->jsn", output_gradient, value_matrix)
    row_delta = jnp.sum(output_gradient * attention_result, axis=-1, keepdims=True)
    score_gradient = (attn_prob * (probability_gradient - row_delta) * logit_scale).astype(jnp.bfloat16).astype(jnp.float32)
    query_gradient = jnp.einsum("gfl,lh->gfh", score_gradient, key_matrix)
    key_gradient = jnp.einsum("uai,uaw->uiw", score_gradient, complete_query)
    value_gradient = jnp.einsum("uai,uaw->uiw", probability_lowered, output_gradient)
    grad_kv = jnp.concatenate([key_gradient[..., :NOPE], value_gradient], axis=-1).astype(jnp.bfloat16).astype(jnp.float32)
    grad_main = jnp.einsum("bkc,rc->kr", grad_kv, head_weight.astype(jnp.float32))
    grad_rope = jnp.sum(key_gradient[..., NOPE:], axis=0)
    grad_weight = jnp.einsum("kr,bkc->rc", latent_main.astype(jnp.float32), grad_kv)
    return attention_result.astype(jnp.bfloat16), query_gradient.astype(jnp.bfloat16), jnp.concatenate([grad_main, grad_rope], axis=1), grad_weight


def reference(latent, queries, up_weight, out_grad, logratio, student_logprob, teacher_logprob, group_order):
    positions = positions_of(group_order, SEQ, GROUP)
    visible = (positions[None, :] <= positions[:, None]).reshape(N_CTX, TOK_DEV, SEQ)
    tok_weight = token_weight(logratio, student_logprob, teacher_logprob).reshape(N_CTX, TOK_DEV)
    q_heads = queries.reshape(N_CTX, TOK_DEV, H, QK).transpose(2, 0, 1, 3)
    g_heads = out_grad.reshape(N_CTX, TOK_DEV, H, VDIM).transpose(2, 0, 1, 3)
    w_heads = up_weight.reshape(KV_RANK, H, NOPE + VDIM).transpose(1, 0, 2)

    def head_step(running, sliced):
        head_query, head_grad, head_weight = sliced
        attention_result, query_gradient, grad_latent, grad_weight = head_block(head_query, head_grad, head_weight, latent, visible, tok_weight)
        return running + grad_latent, (attention_result, query_gradient, grad_weight)

    start_value = jnp.zeros((SEQ, LATENT), jnp.float32)
    latent_grad, stacked = lax.scan(head_step, start_value, (q_heads, g_heads, w_heads))
    attn_output = stacked[0].transpose(1, 2, 0, 3).reshape(SEQ, H * VDIM)
    query_grad = stacked[1].transpose(1, 2, 0, 3).reshape(SEQ, H * QK)
    weight_grad = stacked[2].transpose(1, 0, 2).reshape(KV_RANK, H * (NOPE + VDIM))
    return attn_output, query_grad, latent_grad, weight_grad
```

```python
import functools, math
import jax, jax.numpy as jnp
from jax import lax
from jax.sharding import PartitionSpec as P
from jax.experimental import pallas as pl
from jax.experimental.pallas import tpu as pltpu
NOPE=128; VDIM=128; KV_RANK=512; QK=192; ROPE=64
BF=jnp.bfloat16; F32=jnp.float32
KEYS=2048; ROWS=256; LAT=576
CH=256
SCALE=QK**-0.5
C2=SCALE*math.log2(math.e)
def mm(a,b): return jnp.dot(a,b,preferred_element_type=F32)
def nt(a,b): return lax.dot_general(a,b,(((1,),(1,)),((),())),preferred_element_type=F32)
def tn(a,b): return lax.dot_general(a,b,(((0,),(0,)),((),())),preferred_element_type=F32)

def body(lat_ref,posk_ref,posq_ref,tw_ref,q_ref,g_ref,w_ref,
         out_ref,dq_ref,wg_ref,lt_ref,
         latT,bias,acc,kk,vv,ss,ee,dd,dkv):
    step=pl.program_id(0)
    @pl.when(step==0)
    def _():
        for j in range(KEYS//CH):
            r=pl.ds(j*CH,CH)
            latT[:,r]=lat_ref[r,:KV_RANK].T
            bias[r,:]=jnp.where(posk_ref[r,:]<=posq_ref[...],0.0,-jnp.inf)
            for hh in range(2):
                kk[hh,r,NOPE:]=lat_ref[r,KV_RANK:]
        acc[...]=jnp.zeros_like(acc)
    W=w_ref[...]
    q=q_ref[...]
    qT=q.T
    dout=(tw_ref[...]*g_ref[...].astype(F32)).astype(BF)
    gT=dout.T
    n=KEYS//CH
    mx=[None,None]
    for j in range(n):
        r=pl.ds(j*CH,CH)
        kv=mm(lat_ref[r,:KV_RANK],W).astype(BF)
        b=bias[r,:]
        for hh in range(2):
            kk[hh,r,:NOPE]=kv[:,hh*256:hh*256+NOPE]
            vv[hh,r,:]=kv[:,hh*256+NOPE:hh*256+256]
            s=mm(kk[hh,r,:],qT[hh*QK:(hh+1)*QK])+b
            ss[hh,r,:]=s
            m=jnp.max(s.reshape(CH//8,8,ROWS),axis=0)
            mx[hh]=m if mx[hh] is None else jnp.maximum(mx[hh],m)
    rl=[];delta=[];qs=[];gs=[];gh=[]
    for hh in range(2):
        mc=jnp.max(mx[hh],axis=0,keepdims=True)*C2
        l=jnp.zeros((8,ROWS),F32)
        for j in range(n):
            r=pl.ds(j*CH,CH)
            e=jnp.exp2(ss[hh,r,:]*C2-mc)
            l=l+jnp.sum(e.reshape(CH//8,8,ROWS),axis=0)
            ee[hh,r,:]=e.astype(BF)
        inv=1.0/jnp.sum(l,axis=0,keepdims=True)
        oT=tn(vv[hh],ee[hh])*inv
        g_h=gT[hh*VDIM:(hh+1)*VDIM]
        delta.append(jnp.sum(oT*g_h.astype(F32),axis=0,keepdims=True))
        out_ref[:,hh*VDIM:(hh+1)*VDIM]=oT.T.astype(BF)
        rl.append(inv)
        gh.append(g_h)
        qs.append((qT[hh*QK:(hh+1)*QK].astype(F32)*(inv*SCALE)).astype(BF))
        gs.append((g_h.astype(F32)*inv).astype(BF))
    for j in range(n):
        r=pl.ds(j*CH,CH)
        ropes=None
        for hh in range(2):
            e=ee[hh,r,:]
            dp=mm(vv[hh,r,:],gh[hh])
            ds=(e.astype(F32)*(dp-delta[hh])).astype(BF)
            dd[hh,r,:]=ds
            dk=nt(ds,qs[hh])
            dv=nt(e,gs[hh])
            dkv[r,hh*256:hh*256+NOPE]=dk[:,:NOPE].astype(BF)
            dkv[r,hh*256+NOPE:hh*256+256]=dv.astype(BF)
            ropes=dk[:,NOPE:] if ropes is None else ropes+dk[:,NOPE:]
        acc[r,:KV_RANK]+=nt(dkv[r,:],W)
        acc[r,KV_RANK:]+=ropes
    dqT=[tn(kk[hh],dd[hh])*(rl[hh]*SCALE) for hh in range(2)]
    dq_ref[...]=jnp.concatenate(dqT,axis=0).T.astype(BF)
    wg_ref[...]=mm(latT[...],dkv[...]).astype(BF)
    @pl.when(step==pl.num_programs(0)-1)
    def _():
        lt_ref[...]=acc[...].astype(BF)

def attn(lat,posk,posq,tw,q,g,w):
    full=lambda s: pl.BlockSpec(s,lambda i:(0,0))
    heads=q.shape[1]//QK
    return pl.pallas_call(body,grid=(heads//2,),
        in_specs=[full((KEYS,LAT)),full((KEYS,1)),full((1,ROWS)),full((ROWS,1)),
            pl.BlockSpec((ROWS,2*QK),lambda i:(0,i)),pl.BlockSpec((ROWS,2*VDIM),lambda i:(0,i)),pl.BlockSpec((KV_RANK,512),lambda i:(0,i))],
        out_specs=[pl.BlockSpec((ROWS,2*VDIM),lambda i:(0,i)),pl.BlockSpec((ROWS,2*QK),lambda i:(0,i)),pl.BlockSpec((KV_RANK,512),lambda i:(0,i)),full((KEYS,LAT))],
        out_shape=[jax.ShapeDtypeStruct((ROWS,heads*VDIM),BF),jax.ShapeDtypeStruct((ROWS,heads*QK),BF),jax.ShapeDtypeStruct((KV_RANK,heads*256),BF),jax.ShapeDtypeStruct((KEYS,LAT),BF)],
        scratch_shapes=[pltpu.VMEM((KV_RANK,KEYS),BF),pltpu.VMEM((KEYS,ROWS),F32),pltpu.VMEM((KEYS,LAT),F32),
            pltpu.VMEM((2,KEYS,QK),BF),pltpu.VMEM((2,KEYS,VDIM),BF),pltpu.VMEM((2,KEYS,ROWS),F32),pltpu.VMEM((2,KEYS,ROWS),BF),pltpu.VMEM((2,KEYS,ROWS),BF),pltpu.VMEM((KEYS,512),BF)],
        compiler_params=pltpu.CompilerParams(vmem_limit_bytes=56*2**20),
        cost_estimate=pl.CostEstimate(flops=2*heads*1300*10**6,bytes_accessed=16*2**20,transcendentals=heads*2**19),
    )(lat,posk,posq,tw,q,g,w)


AXES = ("ctx", "head")


def device_index(x, y, z, core):
    return ((y % 2) * 4 + x) * 16 + z * 4 + (y // 2) * 2 + core


def shift_pairs(steps_of_core):
    pairs = []
    for x in range(4):
        for y in range(4):
            for z in range(4):
                for core in range(2):
                    dx, dy, dz = steps_of_core[core]
                    pairs.append(
                        (
                            device_index(x, y, z, core),
                            device_index((x + dx) % 4, (y + dy) % 4, (z + dz) % 4, core),
                        )
                    )
    return pairs


def swap_cores(value):
    return lax.ppermute(value, "head", [(i, i ^ 1) for i in range(16)])


def swap_ylo(value):
    return lax.ppermute(value, "ctx", [(i, (i + 4) % 8) for i in range(8)])


def send_shift(value, first, second):
    return lax.ppermute(value, AXES, shift_pairs((first, second)))


def gather_latent(latent, z, y_hi, core):
    blocks = latent.reshape(4, 2, 2, 16, LAT)
    blocks = lax.dynamic_index_in_dim(blocks, core, 2, False)
    blocks = jnp.roll(blocks, (-z, -y_hi), (0, 1))
    own = blocks.reshape(128, LAT)
    other = swap_ylo(own)
    pair = jnp.stack([own.reshape(4, 2, 16, LAT), other.reshape(4, 2, 16, LAT)], axis=2)
    far = [pair] + [
        send_shift(pair, (-k, 0, 0), (-k, 0, 0)) for k in (1, 2, 3)
    ]
    mine = jnp.stack(far, axis=0)
    zfirst = mine.transpose(1, 0, 2, 3, 4, 5)
    mine = jnp.where(core == 0, mine, zfirst).reshape(1024, LAT)
    return jnp.concatenate([mine, swap_cores(mine)], axis=0)


def row_index(x, y, z, core):
    rel = jnp.arange(1024, dtype=jnp.int32)
    first, second = rel // 256, (rel // 64) % 4
    dyh, dyl, inner = (rel // 32) % 2, (rel // 16) % 2, rel % 16

    def rows(which):
        dx = jnp.where(which == 0, first, second)
        dz = jnp.where(which == 0, second, first)
        xx, zz = (x + dx) % 4, (z + dz) % 4
        yh, yl = (y // 2 + dyh) % 2, (y % 2 + dyl) % 2
        return ((yl * 4 + xx) * 16 + zz * 4 + yh * 2 + which) * 16 + inner

    return jnp.concatenate([rows(core), rows(1 - core)])


def reduce_latent(keep, send):
    part = keep.astype(F32) + swap_cores(send).astype(F32)
    part = part.reshape(4, 256, LAT)
    wire = part.astype(BF)
    part = part[0] + sum(
        send_shift(wire[k], (k, 0, 0), (0, 0, k)).astype(F32) for k in (1, 2, 3)
    )
    part = part.reshape(4, 64, LAT)
    wire = part.astype(BF)
    part = part[0] + sum(
        send_shift(wire[k], (0, 0, k), (k, 0, 0)).astype(F32) for k in (1, 2, 3)
    )
    part = part.reshape(4, 16, LAT)
    wire = part.astype(BF)
    return wire, part


def shift_y(value, flip_hi, flip_lo):
    pairs = []
    for c in range(8):
        for h in range(16):
            pairs.append((c * 16 + h, (c ^ (4 * flip_lo)) * 16 + (h ^ (2 * flip_hi))))
    return lax.ppermute(value, AXES, pairs)


def positions_of(rows, group_order):
    group = rows // 128
    onehot = group[:, None] == jnp.arange(16, dtype=jnp.int32)[None, :]
    return jnp.sum(jnp.where(onehot, group_order[None, :], 0), axis=1) * 128 + rows % 128


def local(
    latent, queries, up_weight, out_grad, logratio, student_logprob, teacher_logprob, group_order
):
    ctx, head = lax.axis_index("ctx"), lax.axis_index("head")
    x, y_lo = ctx % 4, ctx // 4
    z, y_hi, core = head // 4, (head // 2) % 2, head % 2
    y = y_hi * 2 + y_lo
    rows = gather_latent(latent, z, y_hi, core)
    key_pos = positions_of(row_index(x, y, z, core), group_order)
    own_pos = positions_of(ctx * 256 + jnp.arange(256, dtype=jnp.int32), group_order)
    tok_weight = jnp.clip(jnp.exp(logratio), 0.8, 1.25) * (teacher_logprob - student_logprob)
    attn_output, query_grad, weight_terms, latent_terms = attn(
        rows, key_pos[:, None], own_pos[None, :], tok_weight[:, None], queries, out_grad, up_weight
    )
    weight_grad = lax.psum_scatter(weight_terms, "ctx", scatter_dimension=0, tiled=True)
    wire, part = reduce_latent(latent_terms[:1024], latent_terms[1024:])
    latent_grad = (
        part[0]
        + shift_y(wire[1], 0, 1).astype(F32)
        + shift_y(wire[2], 1, 0).astype(F32)
        + shift_y(wire[3], 1, 1).astype(F32)
    )
    return (attn_output, query_grad, latent_grad, weight_grad.astype(F32))


def solution(mesh):
    placed = (
        P("ctx", None),
        P("ctx", "head"),
        P(None, "head"),
        P("ctx", "head"),
        P("ctx"),
        P("ctx"),
        P("ctx"),
        P(),
    )
    return jax.shard_map(
        local,
        mesh=mesh,
        in_specs=placed,
        out_specs=(P("ctx", "head"), P("ctx", "head"), P(AXES, None), P("ctx", "head")),
        check_vma=False,
    )
```

```python
import math

import jax
import jax.numpy as jnp
from jax import lax
from jax.experimental import pallas as pl
from jax.experimental.pallas import tpu as pltpu
from jax.sharding import PartitionSpec as P

NOPE = 128
VDIM = 128
KV_RANK = 512
QK = 192
LAT = 576
KEYS = 2048
ROWS = 256
BF = jnp.bfloat16
F32 = jnp.float32
SCALE = QK ** -0.5
SCALE_LOG2 = SCALE * math.log2(math.e)
AT_QUERY, AT_X, AT_YLO, AT_CORE = 128, 130, 131, 132


def mm(a, b):
    return jnp.dot(a, b, preferred_element_type=F32)


def mm_last(a, b):
    return lax.dot_general(a, b, (((1,), (1,)), ((), ())), preferred_element_type=F32)


def mm_first(a, b):
    return lax.dot_general(a, b, (((0,), (0,)), ((), ())), preferred_element_type=F32)


def prepare(ints, pieces, lat, lat_t, bias, keys):
    for i, piece in enumerate(pieces):
        rows = pl.ds(i * 256, 256)
        lat[rows, :] = piece[:, :KV_RANK]
        for hh in range(2):
            keys[hh, rows, NOPE:] = piece[:, KV_RANK:]
    for block in range(8):
        far = (block // 4 + ints[AT_YLO]) % 2
        slot = far * 4 + (block % 4 - ints[AT_X] + 4) % 4
        start = pl.multiple_of(slot * 64, 64)
        lat_t[pl.ds(start, 64), :] = lat[:, block * 64 : block * 64 + 64].T
    lane = lax.broadcasted_iota(jnp.int32, (16, ROWS), 1)
    query_pos = lane % 128 + jnp.where(lane < 128, ints[AT_QUERY], ints[AT_QUERY + 1])
    query_pos = query_pos - lax.broadcasted_iota(jnp.int32, (16, ROWS), 0)
    for i in range(128):
        bias[i * 16 : i * 16 + 16, :] = jnp.where(ints[i] <= query_pos, 0.0, -jnp.inf)


def head_pair(tw, q, g, w, out, dq, wg_keep, wg_send, lat, lat_t, bias, acc, keys, vals, scores, exps, dscores, dkv):
    q_t = q[...].T
    g_t = (g[...].T.astype(F32) * tw[...]).astype(BF)
    kv = mm(lat[...], w[...]).astype(BF)
    top = []
    for hh in range(2):
        keys[hh, :, :NOPE] = kv[:, hh * 256 : hh * 256 + NOPE]
        vals[hh] = kv[:, hh * 256 + NOPE : hh * 256 + 256]
        s = mm(keys[hh], q_t[hh * QK : hh * QK + QK]) + bias[...]
        scores[hh] = s
        top.append(jnp.max(s, axis=0, keepdims=True) * SCALE_LOG2)
    inverse, delta, q_s, g_s, g_h = [], [], [], [], []
    for hh in range(2):
        e = jnp.exp2(scores[hh] * SCALE_LOG2 - top[hh])
        exps[hh] = e.astype(BF)
        inv = 1.0 / jnp.sum(e, axis=0, keepdims=True)
        o_t = mm_first(vals[hh], exps[hh]) * inv
        gh = g_t[hh * VDIM : hh * VDIM + VDIM]
        delta.append(jnp.sum(o_t * gh.astype(F32), axis=0, keepdims=True))
        out[:, hh * VDIM : hh * VDIM + VDIM] = o_t.T.astype(BF)
        inverse.append(inv)
        g_h.append(gh)
        q_s.append((q_t[hh * QK : hh * QK + QK].astype(F32) * (inv * SCALE)).astype(BF))
        g_s.append((gh.astype(F32) * inv).astype(BF))
    rope = None
    for hh in range(2):
        dp = mm(vals[hh], g_h[hh])
        dscores[hh] = (exps[hh].astype(F32) * (dp - delta[hh])).astype(BF)
        dk = mm_last(dscores[hh], q_s[hh])
        dv = mm_last(exps[hh], g_s[hh])
        dkv[:, hh * 256 : hh * 256 + NOPE] = dk[:, :NOPE].astype(BF)
        dkv[:, hh * 256 + NOPE : hh * 256 + 256] = dv.astype(BF)
        rope = dk[:, NOPE:] if rope is None else rope + dk[:, NOPE:]
    acc[:, :KV_RANK] += mm_last(dkv[...], w[...])
    acc[:, KV_RANK:] += rope
    dq_t = [mm_first(keys[hh], dscores[hh]) * (inverse[hh] * SCALE) for hh in range(2)]
    dq[...] = jnp.concatenate(dq_t, axis=0).T.astype(BF)
    wg = mm(lat_t[...], dkv[...]).astype(BF)
    wg_keep[...] = wg[:256]
    wg_send[...] = wg[256:]


def first_body(ints, *refs):
    pieces, (tw, q, g, w, out, dq, wg_keep, wg_send, partial) = refs[:8], refs[8:17]
    scratch = refs[17:]
    lat, lat_t, bias, acc, keys = scratch[:5]

    @pl.when(pl.program_id(0) == 0)
    def _():
        prepare(ints, pieces, lat, lat_t, bias, keys)
        acc[...] = jnp.zeros_like(acc)

    head_pair(tw, q, g, w, out, dq, wg_keep, wg_send, *scratch)

    @pl.when(pl.program_id(0) == pl.num_programs(0) - 1)
    def _():
        partial[...] = acc[...].astype(BF)


def second_body(ints, *refs):
    pieces, (partial, tw, q, g, w, out, dq, wg_keep, wg_send, keep, send) = refs[:8], refs[10:21]
    scratch = refs[21:]
    lat, lat_t, bias, acc, keys = scratch[:5]

    @pl.when(pl.program_id(0) == 0)
    def _():
        prepare(ints, pieces, lat, lat_t, bias, keys)
        acc[...] = partial[...].astype(F32)

    head_pair(tw, q, g, w, out, dq, wg_keep, wg_send, *scratch)

    @pl.when(pl.program_id(0) == pl.num_programs(0) - 1)
    def _():
        core = ints[AT_CORE]
        for a in range(4):
            for b in range(4):
                x_first, z_first = a * 4 + b, b * 4 + a
                rows = pl.ds(x_first * 64, 64)
                keep[jnp.where(core == 0, x_first, z_first)] = acc[rows, :].astype(BF)
                rows = pl.ds(1024 + x_first * 64, 64)
                send[jnp.where(core == 0, z_first, x_first)] = acc[rows, :].astype(BF)


def attention(ints, pieces, tok_weight, queries, out_grad, up_weight, first_pair, pairs, before=None):
    def whole(shape):
        return pl.BlockSpec(shape, lambda i: (0,) * len(shape))

    def part(rows, columns):
        return pl.BlockSpec((rows, columns), lambda i: (0, i + first_pair))

    def made(rows, columns):
        return pl.BlockSpec((rows, columns), lambda i: (0, i))

    def shape(*dims):
        return jax.ShapeDtypeStruct(dims, BF)

    last = before is not None
    in_specs = [pl.BlockSpec(memory_space=pltpu.SMEM)] + [whole((256, LAT))] * 8
    if last:
        in_specs += [pl.BlockSpec(memory_space=pl.ANY)] * 2 + [whole((KEYS, LAT))]
    in_specs += [whole((1, ROWS)), part(ROWS, 2 * QK), part(ROWS, 2 * VDIM), part(KV_RANK, 512)]
    out_specs = [part(ROWS, 2 * VDIM), part(ROWS, 2 * QK), made(256, 512), made(256, 512)]
    out_shape = [
        shape(*out_grad.shape),
        shape(*queries.shape),
        shape(256, pairs * 512),
        shape(256, pairs * 512),
    ]
    if last:
        out_specs += [whole((16, 64, LAT))] * 2
        out_shape += [shape(16, 64, LAT)] * 2
    else:
        out_specs += [whole((KEYS, LAT))]
        out_shape += [shape(KEYS, LAT)]
    operands = [ints, *pieces] + (list(before) if last else [])
    return pl.pallas_call(
        second_body if last else first_body,
        grid=(pairs,),
        in_specs=in_specs,
        out_specs=out_specs,
        out_shape=out_shape,
        input_output_aliases={9: 0, 10: 1} if last else {},
        scratch_shapes=[
            pltpu.VMEM((KEYS, KV_RANK), BF),
            pltpu.VMEM((KV_RANK, KEYS), BF),
            pltpu.VMEM((KEYS, ROWS), F32),
            pltpu.VMEM((KEYS, LAT), F32),
            pltpu.VMEM((2, KEYS, QK), BF),
            pltpu.VMEM((2, KEYS, VDIM), BF),
            pltpu.VMEM((2, KEYS, ROWS), F32),
            pltpu.VMEM((2, KEYS, ROWS), BF),
            pltpu.VMEM((2, KEYS, ROWS), BF),
            pltpu.VMEM((KEYS, 512), BF),
        ],
        compiler_params=pltpu.CompilerParams(vmem_limit_bytes=56 * 2**20),
        cost_estimate=pl.CostEstimate(
            flops=2 * pairs * 3200 * 10**6, bytes_accessed=8 * 2**20, transcendentals=pairs * 2**20
        ),
    )(*operands, tok_weight, queries, out_grad, up_weight)


AXES = ("ctx", "head")


def device_index(x, y, z, core):
    return ((y % 2) * 4 + x) * 16 + z * 4 + (y // 2) * 2 + core


def send_shift(value, first, second):
    pairs = []
    for x in range(4):
        for y in range(4):
            for z in range(4):
                for core, (dx, dy, dz) in enumerate((first, second)):
                    target = device_index((x + dx) % 4, (y + dy) % 4, (z + dz) % 4, core)
                    pairs.append((device_index(x, y, z, core), target))
    return lax.ppermute(value, AXES, pairs)


def swap_cores(value):
    return lax.ppermute(value, "head", [(i, i ^ 1) for i in range(16)])


def swap_ylo(value):
    return lax.ppermute(value, "ctx", [(i, i ^ 4) for i in range(8)])


def swap_y(value, flip_hi, flip_lo):
    pairs = [
        (c * 16 + h, (c ^ (4 * flip_lo)) * 16 + (h ^ (2 * flip_hi)))
        for c in range(8)
        for h in range(16)
    ]
    return lax.ppermute(value, AXES, pairs)


def gather_latent(latent, z, y_hi, core):
    blocks = lax.dynamic_index_in_dim(latent.reshape(4, 2, 2, 16, LAT), core, 2, False)
    own = jnp.roll(blocks, (-z, -y_hi), (0, 1))
    pair = jnp.stack([own, swap_ylo(own)], axis=2)
    mine = [pair] + [send_shift(pair, (-k, 0, 0), (-k, 0, 0)) for k in (1, 2, 3)]
    other = [swap_cores(piece) for piece in mine]
    return [piece.reshape(256, LAT) for piece in mine + other]


def kernel_ints(x, y_lo, z, y_hi, core, group_order):
    block = jnp.arange(128, dtype=jnp.int32)
    which = core ^ (block // 64)
    far_x, far_z = (x + (block // 16) % 4) % 4, (z + (block // 4) % 4) % 4
    far_hi, far_lo = y_hi ^ ((block // 2) % 2), y_lo ^ (block % 2)
    row = ((far_lo * 4 + far_x) * 16 + far_z * 4 + far_hi * 2 + which) * 16
    groups = jnp.concatenate([row // 128, (y_lo * 4 + x) * 2 + jnp.arange(2, dtype=jnp.int32)])
    onehot = groups[:, None] == jnp.arange(16, dtype=jnp.int32)[None, :]
    starts = jnp.sum(jnp.where(onehot, group_order[None, :], 0), axis=1) * 128
    starts = starts + jnp.concatenate([row % 128, jnp.zeros((2,), jnp.int32)])
    return jnp.concatenate([starts, jnp.stack([x, y_lo, core])])


def sum_terms(first, others):
    total = first.astype(F32)
    for other in others:
        total = total + other.astype(F32)
    return total


def reduce_latent(keep, send):
    part = sum_terms(keep, [swap_cores(send)])
    wire = part.astype(BF)
    part = sum_terms(
        part[:4], [send_shift(wire[4 * k : 4 * k + 4], (k, 0, 0), (0, 0, k)) for k in (2, 1, 3)]
    )
    wire = part.astype(BF)
    part = sum_terms(part[0], [send_shift(wire[k], (0, 0, k), (k, 0, 0)) for k in (2, 1, 3)])
    part = part.reshape(4, 16, LAT)
    wire = part.astype(BF)
    return sum_terms(part[0], [swap_y(wire[k], k // 2, k % 2) for k in (3, 2, 1)])


def local(
    latent, queries, up_weight, out_grad, logratio, student_logprob, teacher_logprob, group_order
):
    ctx, head = lax.axis_index("ctx"), lax.axis_index("head")
    x, y_lo = ctx % 4, ctx // 4
    z, y_hi, core = head // 4, (head // 2) % 2, head % 2
    pieces = gather_latent(latent, z, y_hi, core)
    ints = kernel_ints(x, y_lo, z, y_hi, core, group_order)
    tok_weight = jnp.clip(jnp.exp(logratio), 0.8, 1.25) * (teacher_logprob - student_logprob)
    operands = (ints, pieces, tok_weight[None, :], queries, out_grad, up_weight)
    out_1, dq_1, wg_keep_1, wg_send_1, partial = attention(*operands, 0, 2)
    wg_1 = sum_terms(wg_keep_1, [swap_ylo(wg_send_1)])
    before = (out_1, dq_1, partial)
    attn_output, query_grad, wg_keep_2, wg_send_2, keep, send = attention(*operands, 2, 2, before)
    latent_grad = reduce_latent(keep, send)
    wg_2 = sum_terms(wg_keep_2, [swap_ylo(wg_send_2)])
    wg = jnp.concatenate([wg_1, wg_2], axis=1).reshape(4, 64, 2048)
    wire = wg.astype(BF)
    weight_grad = sum_terms(wg[0], [send_shift(wire[k], (k, 0, 0), (k, 0, 0)) for k in (2, 1, 3)])
    return (attn_output, query_grad, latent_grad, weight_grad)


def solution(mesh):
    placed = (
        P("ctx", None),
        P("ctx", "head"),
        P(None, "head"),
        P("ctx", "head"),
        P("ctx"),
        P("ctx"),
        P("ctx"),
        P(),
    )
    return jax.shard_map(
        local,
        mesh=mesh,
        in_specs=placed,
        out_specs=(P("ctx", "head"), P("ctx", "head"), P(AXES, None), P("ctx", "head")),
        check_vma=False,
    )
```

```python
import math

import jax
import jax.numpy as jnp
from jax import lax
from jax.experimental import pallas as pl
from jax.experimental.pallas import tpu as pltpu
from jax.sharding import PartitionSpec as P

NOPE = 128
VDIM = 128
KV_RANK = 512
QK = 192
LAT = 576
KEYS = 2048
ROWS = 256
BF = jnp.bfloat16
F32 = jnp.float32
SCALE = QK ** -0.5
SCALE_LOG2 = SCALE * math.log2(math.e)
AT_QUERY, AT_X, AT_YLO, AT_Z, AT_CORE = 128, 130, 131, 132, 133


def mm(a, b):
    return jnp.dot(a, b, preferred_element_type=F32)


def mm_last(a, b):
    return lax.dot_general(a, b, (((1,), (1,)), ((), ())), preferred_element_type=F32)


def mm_first(a, b):
    return lax.dot_general(a, b, (((0,), (0,)), ((), ())), preferred_element_type=F32)


def prepare(ints, pieces, lat, lat_t, bias, keys):
    for i, piece in enumerate(pieces):
        rows = pl.ds(i * 256, 256)
        lat[rows, :] = piece[:, :KV_RANK]
        for hh in range(2):
            keys[hh, rows, NOPE:] = piece[:, KV_RANK:]
    for block in range(8):
        far = (block // 4 + ints[AT_YLO]) % 2
        slot = far * 4 + (block % 4 - ints[AT_X] + 4) % 4
        start = pl.multiple_of(slot * 64, 64)
        lat_t[pl.ds(start, 64), :] = lat[:, block * 64 : block * 64 + 64].T
    lane = lax.broadcasted_iota(jnp.int32, (16, ROWS), 1)
    query_pos = lane % 128 + jnp.where(lane < 128, ints[AT_QUERY], ints[AT_QUERY + 1])
    query_pos = query_pos - lax.broadcasted_iota(jnp.int32, (16, ROWS), 0)
    for i in range(128):
        bias[i * 16 : i * 16 + 16, :] = jnp.where(ints[i] <= query_pos, 0.0, -jnp.inf)


def head_pair(tw, q, g, w, out, dq, lat, lat_t, bias, acc, keys, vals, scores, exps, dscores, dkv):
    q_t = q[...].T
    g_t = (g[...].T.astype(F32) * tw[...]).astype(BF)
    kv = mm(lat[...], w[...]).astype(BF)
    top = []
    for hh in range(2):
        keys[hh, :, :NOPE] = kv[:, hh * 256 : hh * 256 + NOPE]
        vals[hh] = kv[:, hh * 256 + NOPE : hh * 256 + 256]
        s = mm(keys[hh], q_t[hh * QK : hh * QK + QK]) + bias[...]
        scores[hh] = s
        top.append(jnp.max(s, axis=0, keepdims=True) * SCALE_LOG2)
    inverse, delta, q_s, g_s, g_h = [], [], [], [], []
    for hh in range(2):
        e = jnp.exp2(scores[hh] * SCALE_LOG2 - top[hh])
        exps[hh] = e.astype(BF)
        inv = 1.0 / jnp.sum(e, axis=0, keepdims=True)
        o_t = mm_first(vals[hh], exps[hh]) * inv
        gh = g_t[hh * VDIM : hh * VDIM + VDIM]
        delta.append(jnp.sum(o_t * gh.astype(F32), axis=0, keepdims=True))
        out[:, hh * VDIM : hh * VDIM + VDIM] = o_t.T.astype(BF)
        inverse.append(inv)
        g_h.append(gh)
        q_s.append((q_t[hh * QK : hh * QK + QK].astype(F32) * (inv * SCALE)).astype(BF))
        g_s.append((gh.astype(F32) * inv).astype(BF))
    rope = None
    for hh in range(2):
        dp = mm(vals[hh], g_h[hh])
        dscores[hh] = (exps[hh].astype(F32) * (dp - delta[hh])).astype(BF)
        dk = mm_last(dscores[hh], q_s[hh])
        dv = mm_last(exps[hh], g_s[hh])
        dkv[:, hh * 256 : hh * 256 + NOPE] = dk[:, :NOPE].astype(BF)
        dkv[:, hh * 256 + NOPE : hh * 256 + 256] = dv.astype(BF)
        rope = dk[:, NOPE:] if rope is None else rope + dk[:, NOPE:]
    acc[:, :KV_RANK] += mm_last(dkv[...], w[...])
    acc[:, KV_RANK:] += rope
    dq_t = [mm_first(keys[hh], dscores[hh]) * (inverse[hh] * SCALE) for hh in range(2)]
    dq[...] = jnp.concatenate(dq_t, axis=0).T.astype(BF)
    return mm(lat_t[...], dkv[...]).astype(BF)


def body(ints, *refs):
    pieces, (tw, q, g, w, out, dq, wg_1, wg_2, keep, send) = refs[:8], refs[8:18]
    scratch = refs[18:]
    lat, lat_t, bias, acc, keys = scratch[:5]
    step = pl.program_id(0)

    @pl.when(step == 0)
    def _():
        prepare(ints, pieces, lat, lat_t, bias, keys)
        acc[...] = jnp.zeros_like(acc)

    wg = head_pair(tw, q, g, w, out, dq, *scratch)

    @pl.when(step < 2)
    def _():
        for slot in range(2):
            wg_1[slot] = wg[slot * 256 : slot * 256 + 256]

    @pl.when(step >= 2)
    def _():
        for slot in range(4):
            for near in range(2):
                rows = near * 256 + slot * 64
                wg_2[slot, near * 64 : near * 64 + 64, :] = wg[rows : rows + 64]

    @pl.when(step == pl.num_programs(0) - 1)
    def _():
        core = ints[AT_CORE]
        for dx in range(4):
            for z in range(4):
                x_first = dx * 4 + z
                z_first = (z - ints[AT_Z] + 4) % 4 * 4 + (dx + ints[AT_X]) % 4
                rows = pl.ds(x_first * 64, 64)
                keep[jnp.where(core == 0, x_first, z_first)] = acc[rows, :].astype(BF)
                rows = pl.ds(1024 + x_first * 64, 64)
                send[jnp.where(core == 0, z_first, x_first)] = acc[rows, :].astype(BF)


def attention(ints, pieces, tok_weight, queries, out_grad, up_weight):
    def whole(shape):
        return pl.BlockSpec(shape, lambda i: (0,) * len(shape))

    def columns(rows, width):
        return pl.BlockSpec((rows, width), lambda i: (0, i))

    def shape(*dims):
        return jax.ShapeDtypeStruct(dims, BF)

    return pl.pallas_call(
        body,
        grid=(4,),
        in_specs=[pl.BlockSpec(memory_space=pltpu.SMEM)]
        + [whole((256, LAT))] * 8
        + [whole((1, ROWS)), columns(ROWS, 2 * QK), columns(ROWS, 2 * VDIM), columns(KV_RANK, 512)],
        out_specs=[
            columns(ROWS, 2 * VDIM),
            columns(ROWS, 2 * QK),
            pl.BlockSpec((2, 256, 512), lambda i: (0, 0, jnp.minimum(i, 1))),
            pl.BlockSpec((4, 128, 512), lambda i: (0, 0, jnp.maximum(i - 2, 0))),
            whole((16, 64, LAT)),
            whole((16, 64, LAT)),
        ],
        out_shape=[
            shape(*out_grad.shape),
            shape(*queries.shape),
            shape(2, 256, 1024),
            shape(4, 128, 1024),
            shape(16, 64, LAT),
            shape(16, 64, LAT),
        ],
        scratch_shapes=[
            pltpu.VMEM((KEYS, KV_RANK), BF),
            pltpu.VMEM((KV_RANK, KEYS), BF),
            pltpu.VMEM((KEYS, ROWS), F32),
            pltpu.VMEM((KEYS, LAT), F32),
            pltpu.VMEM((2, KEYS, QK), BF),
            pltpu.VMEM((2, KEYS, VDIM), BF),
            pltpu.VMEM((2, KEYS, ROWS), F32),
            pltpu.VMEM((2, KEYS, ROWS), BF),
            pltpu.VMEM((2, KEYS, ROWS), BF),
            pltpu.VMEM((KEYS, 512), BF),
        ],
        compiler_params=pltpu.CompilerParams(vmem_limit_bytes=56 * 2**20),
        cost_estimate=pl.CostEstimate(
            flops=26 * 10**9, bytes_accessed=16 * 2**20, transcendentals=2**22
        ),
    )(ints, *pieces, tok_weight, queries, out_grad, up_weight)


AXES = ("ctx", "head")


def device_index(x, y, z, core):
    return ((y % 2) * 4 + x) * 16 + z * 4 + (y // 2) * 2 + core


def send_shift(value, first, second):
    pairs = []
    for x in range(4):
        for y in range(4):
            for z in range(4):
                for core, (dx, dy, dz) in enumerate((first, second)):
                    target = device_index((x + dx) % 4, (y + dy) % 4, (z + dz) % 4, core)
                    pairs.append((device_index(x, y, z, core), target))
    return lax.ppermute(value, AXES, pairs)


def swap_cores(value):
    return lax.ppermute(value, "head", [(i, i ^ 1) for i in range(16)])


def swap_ylo(value):
    return lax.ppermute(value, "ctx", [(i, i ^ 4) for i in range(8)])


def exchange_rest(value):
    groups = [
        [device_index(x, yh * 2 + yl, z, 0) for z in range(4) for yh in range(2) for yl in range(2)]
        for x in range(4)
    ] + [
        [device_index(x, yh * 2 + yl, z, 1) for x in range(4) for yh in range(2) for yl in range(2)]
        for z in range(4)
    ]
    return lax.all_to_all(value, AXES, 0, 0, tiled=True, axis_index_groups=groups)


def gather_latent(latent, y_lo, core):
    own = lax.dynamic_index_in_dim(latent.reshape(4, 2, 2, 16, LAT), core, 2, False)
    other = swap_ylo(own)
    low, high = jnp.where(y_lo == 0, own, other), jnp.where(y_lo == 0, other, own)
    pair = jnp.stack([low, high], axis=2)
    mine = [pair] + [send_shift(pair, (-k, 0, 0), (-k, 0, 0)) for k in (1, 2, 3)]
    other = [swap_cores(piece) for piece in mine]
    return [piece.reshape(256, LAT) for piece in mine + other]


def kernel_ints(x, y_lo, z, core, group_order):
    block = jnp.arange(128, dtype=jnp.int32)
    which = core ^ (block // 64)
    far_x = (x + (block // 16) % 4) % 4
    row = ((block % 2 * 4 + far_x) * 16 + (block // 4) % 4 * 4 + block // 2 % 2 * 2 + which) * 16
    groups = jnp.concatenate([row // 128, (y_lo * 4 + x) * 2 + jnp.arange(2, dtype=jnp.int32)])
    onehot = groups[:, None] == jnp.arange(16, dtype=jnp.int32)[None, :]
    starts = jnp.sum(jnp.where(onehot, group_order[None, :], 0), axis=1) * 128
    starts = starts + jnp.concatenate([row % 128, jnp.zeros((2,), jnp.int32)])
    return jnp.concatenate([starts, jnp.stack([x, y_lo, z, core])])


def sum_terms(first, others):
    total = first.astype(F32)
    for other in others:
        total = total + other.astype(F32)
    return total


def after(value, *earlier):
    return lax.optimization_barrier((value, *earlier))[0]


def reduce_terms(keep, send, wg_1, wg_2):
    def along_x(value):
        return [send_shift(value[k], (k, 0, 0), (k, 0, 0)) for k in (2, 1, 3)]

    swapped = swap_cores(send)
    near_1 = swap_ylo(wg_1[1])
    part = sum_terms(keep, [swapped])
    wire = part.astype(BF)
    terms = [send_shift(wire[4 * k : 4 * k + 4], (k, 0, 0), (0, 0, k)) for k in (2, 1, 3)]
    wg_2 = after(wg_2, wire)
    half_2 = sum_terms(wg_2[0], along_x(wg_2))
    near_2 = swap_ylo(half_2[64:].astype(BF))
    half_1 = sum_terms(wg_1[0], [near_1]).reshape(4, 64, 1024)
    far_1 = along_x(half_1.astype(BF))
    part = sum_terms(part[:4], terms).astype(BF)
    moved = exchange_rest(part.reshape(16, 16, LAT))
    latent_grad = sum_terms(moved[0], [moved[i] for i in range(1, 16)])
    weight_grad = [sum_terms(half_1[0], far_1), sum_terms(half_2[:64], [near_2])]
    return latent_grad, jnp.concatenate(weight_grad, axis=1)


def local(
    latent, queries, up_weight, out_grad, logratio, student_logprob, teacher_logprob, group_order
):
    ctx, head = lax.axis_index("ctx"), lax.axis_index("head")
    x, y_lo, z, core = ctx % 4, ctx // 4, head // 4, head % 2
    pieces = gather_latent(latent, y_lo, core)
    ints = kernel_ints(x, y_lo, z, core, group_order)
    tok_weight = jnp.clip(jnp.exp(logratio), 0.8, 1.25) * (teacher_logprob - student_logprob)
    attn_output, query_grad, wg_1, wg_2, keep, send = attention(
        ints, pieces, tok_weight[None, :], queries, out_grad, up_weight
    )
    latent_grad, weight_grad = reduce_terms(keep, send, wg_1, wg_2)
    return (attn_output, query_grad, latent_grad, weight_grad)


def solution(mesh):
    placed = (
        P("ctx", None),
        P("ctx", "head"),
        P(None, "head"),
        P("ctx", "head"),
        P("ctx"),
        P("ctx"),
        P("ctx"),
        P(),
    )
    return jax.shard_map(
        local,
        mesh=mesh,
        in_specs=placed,
        out_specs=(P("ctx", "head"), P("ctx", "head"), P(AXES, None), P("ctx", "head")),
        check_vma=False,
    )
```

```python
import math

import jax
import jax.numpy as jnp
from jax import lax
from jax.experimental import pallas as pl
from jax.experimental.pallas import tpu as pltpu
from jax.sharding import PartitionSpec as P

NOPE = 128
VDIM = 128
KV_RANK = 512
QK = 192
LAT = 576
KEYS = 2048
ROWS = 512
BF = jnp.bfloat16
F32 = jnp.float32
SCALE = QK ** -0.5
SCALE_LOG2 = SCALE * math.log2(math.e)
AT_QUERY, AT_X, AT_YLO, AT_Z, AT_CORE = 128, 132, 133, 134, 135


def mm(a, b):
    return jnp.dot(a, b, preferred_element_type=F32)


def mm_last(a, b):
    return lax.dot_general(a, b, (((1,), (1,)), ((), ())), preferred_element_type=F32)


def mm_first(a, b):
    return lax.dot_general(a, b, (((0,), (0,)), ((), ())), preferred_element_type=F32)


def prepare(ints, pieces, lat, lat_t, bias, keys):
    for i, piece in enumerate(pieces):
        rows = pl.ds(i * 256, 256)
        lat[rows, :] = piece[:, :KV_RANK]
        for hh in range(2):
            keys[hh, rows, NOPE:] = piece[:, KV_RANK:]
    for block in range(8):
        near = (block // 4 + ints[AT_YLO]) % 2
        start = pl.multiple_of((block % 4 - ints[AT_X] + 4) % 4 * 128 + near * 64, 64)
        lat_t[pl.ds(start, 64), :] = lat[:, block * 64 : block * 64 + 64].T
    lane = lax.broadcasted_iota(jnp.int32, (16, ROWS), 1)
    query_pos = lane % 128 - lax.broadcasted_iota(jnp.int32, (16, ROWS), 0)
    for group in range(4):
        query_pos = query_pos + jnp.where(lane // 128 == group, ints[AT_QUERY + group], 0)
    for i in range(128):
        bias[i * 16 : i * 16 + 16, :] = jnp.where(ints[i] <= query_pos, 0.0, -jnp.inf)


def head_pair(q_t, g_t, w, lat, lat_t, bias, acc, keys, vals, scores, exps, dscores, dkv):
    kv = mm(lat[...], w[...]).astype(BF)
    top = []
    for hh in range(2):
        keys[hh, :, :NOPE] = kv[:, hh * 256 : hh * 256 + NOPE]
        vals[hh] = kv[:, hh * 256 + NOPE : hh * 256 + 256]
        s = mm(keys[hh], q_t[hh * QK : hh * QK + QK]) + bias[...]
        scores[hh] = s
        top.append(jnp.max(s, axis=0, keepdims=True) * SCALE_LOG2)
    out, inverse, delta, q_s, g_s, g_h = [], [], [], [], [], []
    for hh in range(2):
        e = jnp.exp2(scores[hh] * SCALE_LOG2 - top[hh])
        exps[hh] = e.astype(BF)
        inv = 1.0 / jnp.sum(e, axis=0, keepdims=True)
        o_t = mm_first(vals[hh], exps[hh]) * inv
        gh = g_t[hh * VDIM : hh * VDIM + VDIM]
        delta.append(jnp.sum(o_t * gh.astype(F32), axis=0, keepdims=True))
        out.append(o_t)
        inverse.append(inv)
        g_h.append(gh)
        q_s.append((q_t[hh * QK : hh * QK + QK].astype(F32) * (inv * SCALE)).astype(BF))
        g_s.append((gh.astype(F32) * inv).astype(BF))
    rope = None
    for hh in range(2):
        dp = mm(vals[hh], g_h[hh])
        dscores[hh] = (exps[hh].astype(F32) * (dp - delta[hh])).astype(BF)
        dk = mm_last(dscores[hh], q_s[hh])
        dv = mm_last(exps[hh], g_s[hh])
        dkv[:, hh * 256 : hh * 256 + NOPE] = dk[:, :NOPE].astype(BF)
        dkv[:, hh * 256 + NOPE : hh * 256 + 256] = dv.astype(BF)
        rope = dk[:, NOPE:] if rope is None else rope + dk[:, NOPE:]
    acc[:, :KV_RANK] += mm_last(dkv[...], w[...])
    acc[:, KV_RANK:] += rope
    dq_t = [mm_first(keys[hh], dscores[hh]) * (inverse[hh] * SCALE) for hh in range(2)]
    out = jnp.concatenate(out, axis=0).T.astype(BF)
    dq = jnp.concatenate(dq_t, axis=0).T.astype(BF)
    return out, dq, mm(lat_t[...], dkv[...]).astype(BF)


def body(ints, *refs):
    pieces, (q, g, far_q, far_g, w, out, dq, far_out, wg_0, wg_1, wg_2, wg_3, keep, send) = (
        refs[:8],
        refs[8:22],
    )
    scratch = refs[22:]
    lat, lat_t, bias, acc, keys = scratch[:5]
    step = pl.program_id(0)

    @pl.when(step == 0)
    def _():
        prepare(ints, pieces, lat, lat_t, bias, keys)
        acc[...] = jnp.zeros_like(acc)

    q_t = jnp.concatenate([q[...].T, far_q[...].T], axis=1)
    g_t = jnp.concatenate([g[...].T, far_g[...].T], axis=1)
    out_pair, dq_pair, wg = head_pair(q_t, g_t, w, *scratch)
    out[...] = out_pair[:256]
    dq[...] = dq_pair[:256]
    for k, ref in enumerate((wg_0, wg_1, wg_2, wg_3)):
        ref[...] = wg[k * 128 : k * 128 + 128]
    for i in range(2):

        @pl.when(step == i)
        def _():
            far_out[:, i * 2 * QK : (i + 1) * 2 * QK] = dq_pair[256:]
            far_out[:, 4 * QK + i * 2 * VDIM : 4 * QK + (i + 1) * 2 * VDIM] = out_pair[256:]

    @pl.when(step == pl.num_programs(0) - 1)
    def _():
        core = ints[AT_CORE]
        for dx in range(4):
            for z in range(4):
                x_first = dx * 4 + z
                z_first = (z - ints[AT_Z] + 4) % 4 * 4 + (dx + ints[AT_X]) % 4
                rows = pl.ds(x_first * 64, 64)
                keep[jnp.where(core == 0, x_first, z_first)] = acc[rows, :].astype(BF)
                rows = pl.ds(1024 + x_first * 64, 64)
                send[jnp.where(core == 0, z_first, x_first)] = acc[rows, :].astype(BF)


def attention(ints, pieces, queries, out_grad, far, up_weight):
    def whole(*dims):
        return pl.BlockSpec(dims, lambda i, n: (0,) * len(dims))

    def once(*dims):
        return pl.BlockSpec(dims, lambda i, n: (0,) * len(dims), pipeline_mode=pl.Buffered(1))

    def mine(rows, width):
        return pl.BlockSpec((rows, width), lambda i, n: (0, i + 2 * n[AT_YLO]))

    def columns(rows, width, first=0):
        return pl.BlockSpec((rows, width), lambda i, n: (0, i + first))

    def shape(*dims):
        return jax.ShapeDtypeStruct(dims, BF)

    return pl.pallas_call(
        body,
        grid_spec=pltpu.PrefetchScalarGridSpec(
            num_scalar_prefetch=1,
            grid=(2,),
            in_specs=[once(256, LAT)] * 8
            + [
                mine(256, 2 * QK),
                mine(256, 2 * VDIM),
                columns(256, 2 * QK),
                columns(256, 2 * VDIM, 3),
                mine(KV_RANK, 512),
            ],
            out_specs=[
                columns(256, 2 * VDIM),
                columns(256, 2 * QK),
                whole(256, 4 * (QK + VDIM)),
                columns(128, 512),
                columns(128, 512),
                columns(128, 512),
                columns(128, 512),
                whole(16, 64, LAT),
                whole(16, 64, LAT),
            ],
            scratch_shapes=[
                pltpu.VMEM((KEYS, KV_RANK), BF),
                pltpu.VMEM((KV_RANK, KEYS), BF),
                pltpu.VMEM((KEYS, ROWS), F32),
                pltpu.VMEM((KEYS, LAT), F32),
                pltpu.VMEM((2, KEYS, QK), BF),
                pltpu.VMEM((2, KEYS, VDIM), BF),
                pltpu.VMEM((2, KEYS, ROWS), F32),
                pltpu.VMEM((2, KEYS, ROWS), BF),
                pltpu.VMEM((2, KEYS, ROWS), BF),
                pltpu.VMEM((KEYS, 512), BF),
            ],
        ),
        out_shape=[
            shape(256, 4 * VDIM),
            shape(256, 4 * QK),
            shape(256, 4 * (QK + VDIM)),
            shape(128, 1024),
            shape(128, 1024),
            shape(128, 1024),
            shape(128, 1024),
            shape(16, 64, LAT),
            shape(16, 64, LAT),
        ],
        compiler_params=pltpu.CompilerParams(vmem_limit_bytes=60 * 2**20),
        cost_estimate=pl.CostEstimate(
            flops=20 * 10**9, bytes_accessed=16 * 2**20, transcendentals=2**22
        ),
    )(ints, *pieces, queries, out_grad, far, far, up_weight)


AXES = ("ctx", "head")


def device_index(x, y, z, core):
    return ((y % 2) * 4 + x) * 16 + z * 4 + (y // 2) * 2 + core


def send_shift(value, first, second):
    pairs = []
    for x in range(4):
        for y in range(4):
            for z in range(4):
                for core, (dx, dy, dz) in enumerate((first, second)):
                    target = device_index((x + dx) % 4, (y + dy) % 4, (z + dz) % 4, core)
                    pairs.append((device_index(x, y, z, core), target))
    return lax.ppermute(value, AXES, pairs)


def swap_cores(value):
    return lax.ppermute(value, "head", [(i, i ^ 1) for i in range(16)])


def swap_ylo(value):
    return lax.ppermute(value, "ctx", [(i, i ^ 4) for i in range(8)])


def exchange_rest(value):
    groups = [
        [device_index(x, yh * 2 + yl, z, 0) for z in range(4) for yh in range(2) for yl in range(2)]
        for x in range(4)
    ] + [
        [device_index(x, yh * 2 + yl, z, 1) for x in range(4) for yh in range(2) for yl in range(2)]
        for z in range(4)
    ]
    return lax.all_to_all(value, AXES, 0, 0, tiled=True, axis_index_groups=groups)


def gather_latent(latent, y_lo, core):
    own = lax.dynamic_index_in_dim(latent.reshape(4, 2, 2, 16, LAT), core, 2, False)
    other = swap_ylo(own)
    low, high = jnp.where(y_lo == 0, own, other), jnp.where(y_lo == 0, other, own)
    pair = jnp.stack([low, high], axis=2)
    mine = [pair] + [send_shift(pair, (-k, 0, 0), (-k, 0, 0)) for k in (1, 2, 3)]
    other = [swap_cores(piece) for piece in mine]
    return [piece.reshape(256, LAT) for piece in mine + other]


def kernel_ints(x, y_lo, z, core, group_order):
    block = jnp.arange(128, dtype=jnp.int32)
    which = core ^ (block // 64)
    far_x = (x + (block // 16) % 4) % 4
    row = ((block % 2 * 4 + far_x) * 16 + (block // 4) % 4 * 4 + block // 2 % 2 * 2 + which) * 16
    query = jnp.arange(4, dtype=jnp.int32)
    query = ((y_lo ^ (query // 2)) * 4 + x) * 2 + query % 2
    groups = jnp.concatenate([row // 128, query])
    onehot = groups[:, None] == jnp.arange(16, dtype=jnp.int32)[None, :]
    starts = jnp.sum(jnp.where(onehot, group_order[None, :], 0), axis=1) * 128
    starts = starts + jnp.concatenate([row % 128, jnp.zeros((4,), jnp.int32)])
    return jnp.concatenate([starts, jnp.stack([x, y_lo, z, core])])


def sum_terms(first, others):
    total = first.astype(F32)
    for other in others:
        total = total + other.astype(F32)
    return total


def halves(y_lo, near, far, axis=1):
    low, high = jnp.where(y_lo == 0, near, far), jnp.where(y_lo == 0, far, near)
    return jnp.concatenate([low, high], axis=axis)


def other_half(y_lo, value):
    width = value.shape[1] // 2
    return jnp.where(y_lo == 0, value[:, width:], value[:, :width])


def reduce_terms(y_lo, keep, send, wg, far_out):
    swapped = swap_cores(send)
    far_out = swap_ylo(far_out)
    part = sum_terms(keep, [swapped])
    wire = part.astype(BF)
    terms = [send_shift(wire[4 * k : 4 * k + 4], (k, 0, 0), (0, 0, k)) for k in (2, 1, 3)]
    parts = lax.optimization_barrier((wire, wg[1], wg[2], wg[3]))
    wg_terms = [send_shift(parts[k], (k, 0, 0), (k, 0, 0)) for k in (2, 1, 3)]
    part = sum_terms(part[:4], terms).astype(BF)
    far_out, *wg_terms = lax.optimization_barrier((part, far_out, *wg_terms))[1:]
    wg_sum = sum_terms(wg[0], wg_terms)
    wg_far = swap_ylo(wg_sum[64:].astype(BF))
    moved = exchange_rest(part.reshape(16, 16, LAT))
    latent_grad = sum_terms(moved[0], [moved[i] for i in range(1, 16)])
    return latent_grad, halves(y_lo, wg_sum[:64], wg_far.astype(F32)), far_out


def local(
    latent, queries, up_weight, out_grad, logratio, student_logprob, teacher_logprob, group_order
):
    ctx, head = lax.axis_index("ctx"), lax.axis_index("head")
    x, y_lo, z, core = ctx % 4, ctx // 4, head // 4, head % 2
    pieces = gather_latent(latent, y_lo, core)
    tok_weight = jnp.clip(jnp.exp(logratio), 0.8, 1.25) * (teacher_logprob - student_logprob)
    dout = (tok_weight[:, None] * out_grad.astype(F32)).astype(BF)
    far = swap_ylo(jnp.concatenate([other_half(y_lo, queries), other_half(y_lo, dout)], axis=1))
    ints = kernel_ints(x, y_lo, z, core, group_order)
    out, dq, far_out, wg_0, wg_1, wg_2, wg_3, keep, send = attention(
        ints, pieces, queries, dout, far, up_weight
    )
    latent_grad, weight_grad, far_out = reduce_terms(
        y_lo, keep, send, (wg_0, wg_1, wg_2, wg_3), far_out
    )
    query_grad = halves(y_lo, dq, far_out[:, : 4 * QK])
    attn_output = halves(y_lo, out, far_out[:, 4 * QK :])
    return (attn_output, query_grad, latent_grad, weight_grad)


def solution(mesh):
    placed = (
        P("ctx", None),
        P("ctx", "head"),
        P(None, "head"),
        P("ctx", "head"),
        P("ctx"),
        P("ctx"),
        P("ctx"),
        P(),
    )
    return jax.shard_map(
        local,
        mesh=mesh,
        in_specs=placed,
        out_specs=(P("ctx", "head"), P("ctx", "head"), P(AXES, None), P("ctx", "head")),
        check_vma=False,
    )
```

```python
import math

import jax
import jax.numpy as jnp
from jax import lax
from jax.experimental import pallas as pl
from jax.experimental.pallas import tpu as pltpu
from jax.sharding import PartitionSpec as P

NOPE = 128
VDIM = 128
KV_RANK = 512
QK = 192
LAT = 576
KEYS = 2048
ROWS = 512
CHUNK = 512
BF = jnp.bfloat16
F32 = jnp.float32
SCALE = QK ** -0.5
SCALE_LOG2 = SCALE * math.log2(math.e)
AT_QUERY, AT_WEIGHT, AT_TERM, AT_YLO = 128, 132, 140, 204


def mm(a, b):
    return jnp.dot(a, b, preferred_element_type=F32)


def mm_last(a, b):
    return lax.dot_general(a, b, (((1,), (1,)), ((), ())), preferred_element_type=F32)


def mm_first(a, b):
    return lax.dot_general(a, b, (((0,), (0,)), ((), ())), preferred_element_type=F32)


def prepare(ints, lat, lat_t, bias, keys):
    for hh in range(4):
        keys[hh, :, NOPE:] = lat[:, KV_RANK:]
    for block in range(8):
        start = pl.multiple_of(ints[AT_WEIGHT + block], 64)
        lat_t[pl.ds(start, 64), :] = lat[:, block * 64 : block * 64 + 64].T
    lane = lax.broadcasted_iota(jnp.int32, (16, ROWS), 1)
    query_pos = lane % 128 - lax.broadcasted_iota(jnp.int32, (16, ROWS), 0)
    for group in range(4):
        query_pos = query_pos + jnp.where(lane // 128 == group, ints[AT_QUERY + group], 0)
    for i in range(128):
        bias[i * 16 : i * 16 + 16, :] = jnp.where(ints[i] <= query_pos, 0.0, -jnp.inf)


def body(ints, *refs):
    pieces, (q_hbm, g_hbm, far_hbm, w_hbm) = refs[:8], refs[8:12]
    out_hbm, dq_hbm, far_out_hbm, wg_keep_hbm, wg_send_hbm, keep_hbm, send_hbm = refs[12:19]
    lat, q, g, far, w, lat_t, bias, keys, vals, scores, exps, dscores, dkv, rope = refs[19:33]
    out_b, dq_b, far_out, wg_b, keep, send, sems = refs[33:]
    used = []

    def copy(source, target):
        handle = pltpu.make_async_copy(source, target, sems.at[len(used)])
        used.append(handle)
        handle.start()
        return handle

    y_lo = ints[AT_YLO]
    loads = [copy(w_hbm.at[:, pl.ds(pl.multiple_of(y_lo * 1024, 1024), 1024)], w)]
    loads += [copy(piece, lat.at[pl.ds(i * 256, 256), :]) for i, piece in enumerate(pieces)]
    loads += [
        copy(q_hbm.at[:, pl.ds(pl.multiple_of(y_lo * 768, 256), 768)], q),
        copy(g_hbm.at[:, pl.ds(pl.multiple_of(y_lo * 512, 512), 512)], g),
        copy(far_hbm, far),
    ]
    for load in loads:
        load.wait()
    prepare(ints, lat, lat_t, bias, keys)

    chunks = [pl.ds(c * CHUNK, CHUNK) for c in range(KEYS // CHUNK)]
    q_t = jnp.concatenate([q[...].T, far[:, : 4 * QK].T], axis=1)
    g_t = jnp.concatenate([g[...].T, far[:, 4 * QK :].T], axis=1)
    q_h = [q_t[hh * QK : hh * QK + QK] for hh in range(4)]
    g_h = [g_t[hh * VDIM : hh * VDIM + VDIM] for hh in range(4)]
    top, norm, out, inverse, delta, q_s, g_s, dq = ([None] * 4 for _ in range(8))

    def project(pair, r):
        kv = mm(lat[r, :KV_RANK], w[:, pair * 512 : pair * 512 + 512]).astype(BF)
        for hh in range(2):
            keys[pair * 2 + hh, r, :NOPE] = kv[:, hh * 256 : hh * 256 + NOPE]
            vals[pair * 2 + hh, r, :] = kv[:, hh * 256 + NOPE : hh * 256 + 256]

    def score(hh, r):
        s = mm(keys[hh, r, :], q_h[hh]) + bias[r, :]
        scores[hh % 2, r, :] = s
        high = jnp.max(s.reshape(CHUNK // 8, 8, ROWS), axis=0)
        top[hh] = high if top[hh] is None else jnp.maximum(top[hh], high)

    def close_score(hh):
        top[hh] = jnp.max(top[hh], axis=0, keepdims=True) * SCALE_LOG2

    def weigh(hh, r):
        e = jnp.exp2(scores[hh % 2, r, :] * SCALE_LOG2 - top[hh])
        low = e.astype(BF)
        exps[hh % 2, r, :] = low
        total = jnp.sum(e.reshape(CHUNK // 8, 8, ROWS), axis=0)
        norm[hh] = total if norm[hh] is None else norm[hh] + total
        o_t = mm_first(vals[hh, r, :], low)
        out[hh] = o_t if out[hh] is None else out[hh] + o_t

    def close_weigh(hh):
        inv = 1.0 / jnp.sum(norm[hh], axis=0, keepdims=True)
        out[hh] = out[hh] * inv
        delta[hh] = jnp.sum(out[hh] * g_h[hh].astype(F32), axis=0, keepdims=True)
        inverse[hh] = inv
        q_s[hh] = (q_h[hh].astype(F32) * (inv * SCALE)).astype(BF)
        g_s[hh] = (g_h[hh].astype(F32) * inv).astype(BF)

    def back(hh, r):
        e = exps[hh % 2, r, :]
        dp = mm(vals[hh, r, :], g_h[hh])
        ds = (e.astype(F32) * (dp - delta[hh])).astype(BF)
        dscores[hh % 2, r, :] = ds
        dk = mm_last(ds, q_s[hh])
        dv = mm_last(e, g_s[hh])
        dkv[r, hh * 256 : hh * 256 + NOPE] = dk[:, :NOPE].astype(BF)
        dkv[r, hh * 256 + NOPE : hh * 256 + 256] = dv.astype(BF)
        if hh == 0:
            rope[r, :] = dk[:, NOPE:]
        else:
            rope[r, :] += dk[:, NOPE:]

    def query_grad(hh):
        dq[hh] = mm_first(keys[hh], dscores[hh % 2]) * (inverse[hh] * SCALE)

    def finish(pair):
        columns = slice(pair * 256, pair * 256 + 256)
        value = jnp.concatenate(out[pair * 2 : pair * 2 + 2], axis=0).T.astype(BF)
        out_b[:, columns] = value[:256]
        far_out[:, 768 + pair * 256 : 1024 + pair * 256] = value[256:]
        copy(out_b.at[:, columns], out_hbm.at[:, columns])
        columns = slice(pair * 384, pair * 384 + 384)
        value = jnp.concatenate(dq[pair * 2 : pair * 2 + 2], axis=0).T.astype(BF)
        dq_b[:, columns] = value[:256]
        far_out[:, columns] = value[256:]
        copy(dq_b.at[:, columns], dq_hbm.at[:, columns])
        columns = slice(pair * 512, pair * 512 + 512)
        wg = mm(lat_t[...], dkv[:, columns]).astype(BF)
        for k, target in enumerate((wg_keep_hbm, wg_send_hbm)):
            wg_b[k, :, columns] = wg[k * 256 : k * 256 + 256]
            copy(wg_b.at[k, :, columns], target.at[:, columns])

    def latent_terms(c):
        terms = mm_last(dkv[chunks[c], :], w[...]).astype(BF)
        tail = rope[chunks[c], :].astype(BF)
        for i in range(CHUNK // 32):
            block = c * (CHUNK // 32) + i
            index, target = ints[AT_TERM + block], keep if block < 32 else send
            target[index, :, :KV_RANK] = terms[i * 32 : i * 32 + 32]
            target[index, :, KV_RANK:] = tail[i * 32 : i * 32 + 32]

    for r in chunks:
        project(0, r)
        score(0, r)
    close_score(0)
    for r in chunks:
        score(1, r)
        weigh(0, r)
    close_score(1)
    close_weigh(0)
    for r in chunks:
        back(0, r)
        weigh(1, r)
    close_weigh(1)
    for r in chunks:
        back(1, r)
        project(1, r)
        score(2, r)
    close_score(2)
    query_grad(0)
    for r in chunks:
        score(3, r)
        weigh(2, r)
    close_score(3)
    close_weigh(2)
    query_grad(1)
    finish(0)
    for r in chunks:
        back(2, r)
        weigh(3, r)
    close_weigh(3)
    query_grad(2)
    order = list(range(len(chunks)))
    order = order[len(order) // 2 :] + order[: len(order) // 2]
    for c in order:
        back(3, chunks[c])
        latent_terms(c)
        if c == len(chunks) - 1:
            copy(send, send_hbm)
    copy(keep, keep_hbm)
    query_grad(3)
    finish(1)
    copy(far_out, far_out_hbm)
    for store in used[len(loads) :]:
        store.wait()


def attention(ints, pieces, queries, out_grad, far, up_weight):
    def shape(*dims):
        return jax.ShapeDtypeStruct(dims, BF)

    anywhere = pl.BlockSpec(memory_space=pl.ANY)
    return pl.pallas_call(
        body,
        in_specs=[pl.BlockSpec(memory_space=pltpu.SMEM)] + [anywhere] * 12,
        out_specs=[anywhere] * 7,
        out_shape=[
            shape(256, 4 * VDIM),
            shape(256, 4 * QK),
            shape(256, 4 * (QK + VDIM)),
            shape(256, 1024),
            shape(256, 1024),
            shape(32, 32, LAT),
            shape(32, 32, LAT),
        ],
        scratch_shapes=[
            pltpu.VMEM((KEYS, LAT), BF),
            pltpu.VMEM((256, 4 * QK), BF),
            pltpu.VMEM((256, 4 * VDIM), BF),
            pltpu.VMEM((256, 4 * (QK + VDIM)), BF),
            pltpu.VMEM((KV_RANK, 1024), BF),
            pltpu.VMEM((KV_RANK, KEYS), BF),
            pltpu.VMEM((KEYS, ROWS), F32),
            pltpu.VMEM((4, KEYS, QK), BF),
            pltpu.VMEM((4, KEYS, VDIM), BF),
            pltpu.VMEM((2, KEYS, ROWS), F32),
            pltpu.VMEM((2, KEYS, ROWS), BF),
            pltpu.VMEM((2, KEYS, ROWS), BF),
            pltpu.VMEM((KEYS, 1024), BF),
            pltpu.VMEM((KEYS, QK - NOPE), F32),
            pltpu.VMEM((256, 4 * VDIM), BF),
            pltpu.VMEM((256, 4 * QK), BF),
            pltpu.VMEM((256, 4 * (QK + VDIM)), BF),
            pltpu.VMEM((2, 256, 1024), BF),
            pltpu.VMEM((32, 32, LAT), BF),
            pltpu.VMEM((32, 32, LAT), BF),
            pltpu.SemaphoreType.DMA((32,)),
        ],
        compiler_params=pltpu.CompilerParams(vmem_limit_bytes=53 * 2**20),
        cost_estimate=pl.CostEstimate(
            flops=20 * 10**9, bytes_accessed=16 * 2**20, transcendentals=2**22
        ),
    )(ints, *pieces, queries, out_grad, far, up_weight)


AXES = ("ctx", "head")


def device_index(x, y, z, core):
    return ((y % 2) * 4 + x) * 16 + z * 4 + (y // 2) * 2 + core


def trade(value, first, second):
    pairs = []
    for x in range(4):
        for y in range(4):
            for z in range(4):
                for core, (a, b, c) in enumerate((first, second)):
                    pairs.append((device_index(x, y, z, core), device_index(x ^ a, y ^ b, z ^ c, core)))
    return lax.ppermute(value, AXES, pairs)


def swap_cores(value):
    return lax.ppermute(value, "head", [(i, i ^ 1) for i in range(16)])


def swap_ylo(value):
    return trade(value, (0, 1, 0), (0, 1, 0))


def shift(value, first, second):
    pairs = []
    for x in range(4):
        for y in range(4):
            for z in range(4):
                for core, (a, c) in enumerate((first, second)):
                    target = device_index((x + a) % 4, y, (z + c) % 4, core)
                    pairs.append((device_index(x, y, z, core), target))
    return lax.ppermute(value, AXES, pairs)


def exchange_rest(value):
    groups = [
        [device_index(x, yh * 2 + yl, z, 0) for z in range(4) for yl in range(2) for yh in range(2)]
        for x in range(4)
    ] + [
        [device_index(x, yh * 2 + yl, z, 1) for x in range(4) for yl in range(2) for yh in range(2)]
        for z in range(4)
    ]
    return lax.all_to_all(value, AXES, 0, 0, tiled=True, axis_index_groups=groups)


def gather_latent(latent, core):
    blocks = latent.reshape(4, 2, 2, 16, LAT)
    own = jnp.where(core == 0, blocks[:, :, 0], blocks[:, :, 1])
    pair = jnp.stack([own, swap_ylo(own)], axis=0)
    far = {k: shift(pair, (-k, 0), (-k, 0)) for k in (1, 3, 2)}
    mine = [pair, far[1], far[2], far[3]]
    return [piece.reshape(256, LAT) for piece in mine + [swap_cores(piece) for piece in mine]]


def kernel_ints(x, y_lo, z, core, group_order):
    def key_blocks(rel):
        return (x + rel // 2) % 4, y_lo ^ (rel % 2)

    block = jnp.arange(128, dtype=jnp.int32)
    which = core ^ (block // 64)
    far_x, far_y = key_blocks(block // 8 % 8)
    row = ((far_y * 4 + far_x) * 16 + block // 2 % 4 * 4 + block % 2 * 2 + which) * 16
    query = jnp.arange(4, dtype=jnp.int32)
    query = ((y_lo ^ (query // 2)) * 4 + x) * 2 + query % 2
    groups = jnp.concatenate([row // 128, query])
    onehot = groups[:, None] == jnp.arange(16, dtype=jnp.int32)[None, :]
    starts = jnp.sum(jnp.where(onehot, group_order[None, :], 0), axis=1) * 128
    starts = starts + jnp.concatenate([row % 128, jnp.zeros((4,), jnp.int32)])
    block = jnp.arange(8, dtype=jnp.int32)
    gap = (block % 4) ^ x
    slot = jnp.where(core == 0, (gap ^ gap // 2) % 2 * 2 + gap // 2, gap ^ (gap // 2))
    weight_rows = slot * 128 + ((block // 4) ^ y_lo) * 64
    block = jnp.arange(64, dtype=jnp.int32)
    far_x, far_y = key_blocks(block // 4 % 8)
    far_z = block % 4
    x_first = block // 8 % 4 * 8 + far_z * 2 + far_y
    z_first = (far_z - z + 4) % 4 * 8 + far_x * 2 + far_y
    terms = jnp.where((core ^ (block // 32)) == 0, x_first, z_first)
    return jnp.concatenate([starts, weight_rows, terms, y_lo[None]])


def sum_terms(first, others):
    total = first.astype(F32)
    for other in others:
        total = total + other.astype(F32)
    return total


def halves(y_lo, near, far, axis=1):
    low, high = jnp.where(y_lo == 0, near, far), jnp.where(y_lo == 0, far, near)
    return jnp.concatenate([low, high], axis=axis)


def other_half(y_lo, value):
    width = value.shape[1] // 2
    return jnp.where(y_lo == 0, value[:, width:], value[:, :width])


def reduce_terms(y_lo, out, dq, far_out, wg_keep, wg_send, keep, send):
    swapped = swap_cores(send)
    far_out = swap_ylo(far_out)
    wg_near = trade(wg_send, (1, 0, 0), (3, 0, 0))
    wire = [sum_terms(keep[8 * k : 8 * k + 8], [swapped[8 * k : 8 * k + 8]]) for k in range(4)]
    terms = [shift(wire[k].astype(BF), (k, 0), (0, k)) for k in (2, 1, 3)]
    wg_near = lax.optimization_barrier((wg_near, *wire))[0]
    wg_sum = sum_terms(wg_keep, [wg_near]).reshape(2, 2, 64, 1024)
    wire_wg = wg_sum.astype(BF)
    wg_terms = (
        trade(wire_wg[1, 0], (3, 0, 0), (1, 0, 0)),
        trade(wire_wg[1, 1], (3, 1, 0), (1, 1, 0)),
        swap_ylo(wire_wg[0, 1]),
    )
    part = sum_terms(wire[0], terms).astype(BF)
    far_out, wg_x, wg_xy, wg_y = lax.optimization_barrier((part, far_out, *wg_terms))[1:]
    moved = exchange_rest(part.reshape(16, 16, LAT))
    wg = halves(y_lo, sum_terms(wg_sum[0, 0], [wg_x]), sum_terms(wg_y, [wg_xy]))
    query_grad = halves(y_lo, dq, far_out[:, : 4 * QK])
    attn_output = halves(y_lo, out, far_out[:, 4 * QK :])
    latent_grad = sum_terms(moved[0], [moved[i] for i in range(1, 16)])
    return attn_output, query_grad, latent_grad, wg


def local(
    latent, queries, up_weight, out_grad, logratio, student_logprob, teacher_logprob, group_order
):
    ctx, head = lax.axis_index("ctx"), lax.axis_index("head")
    x, y_lo, z, core = ctx % 4, ctx // 4, head // 4, head % 2
    tok_weight = jnp.clip(jnp.exp(logratio), 0.8, 1.25) * (teacher_logprob - student_logprob)
    dout = (tok_weight[:, None] * out_grad.astype(F32)).astype(BF)
    far = jnp.concatenate([other_half(y_lo, queries), other_half(y_lo, dout)], axis=1)
    far = swap_ylo(far)
    pieces = gather_latent(latent, core)
    ints = kernel_ints(x, y_lo, z, core, group_order)
    results = attention(ints, pieces, queries, dout, far, up_weight)
    return reduce_terms(y_lo, *results)


def solution(mesh):
    placed = (
        P("ctx", None),
        P("ctx", "head"),
        P(None, "head"),
        P("ctx", "head"),
        P("ctx"),
        P("ctx"),
        P("ctx"),
        P(),
    )
    return jax.shard_map(
        local,
        mesh=mesh,
        in_specs=placed,
        out_specs=(P("ctx", "head"), P("ctx", "head"), P(AXES, None), P("ctx", "head")),
        check_vma=False,
    )
```

```python
import math

import jax
import jax.numpy as jnp
from jax import lax
from jax.experimental import pallas as pl
from jax.experimental.pallas import tpu as pltpu
from jax.sharding import PartitionSpec as P

NOPE = 128
VDIM = 128
KV_RANK = 512
QK = 192
LAT = 576
KEYS = 2048
ROWS = 512
CHUNK = 512
BF = jnp.bfloat16
F32 = jnp.float32
SCALE = QK ** -0.5
SCALE_LOG2 = SCALE * math.log2(math.e)
AT_QUERY, AT_WEIGHT, AT_TERM, AT_YLO = 128, 132, 140, 204


def mm(a, b):
    return jnp.dot(a, b, preferred_element_type=F32)


def mm_last(a, b):
    return lax.dot_general(a, b, (((1,), (1,)), ((), ())), preferred_element_type=F32)


def mm_first(a, b):
    return lax.dot_general(a, b, (((0,), (0,)), ((), ())), preferred_element_type=F32)


def prepare(ints, lat, lat_t, bias, keys):
    for hh in range(4):
        keys[hh, :, NOPE:] = lat[:, KV_RANK:]
    for block in range(8):
        start = pl.multiple_of(ints[AT_WEIGHT + block], 64)
        lat_t[pl.ds(start, 64), :] = lat[:, block * 64 : block * 64 + 64].T
    lane = lax.broadcasted_iota(jnp.int32, (16, ROWS), 1)
    query_pos = lane % 128 - lax.broadcasted_iota(jnp.int32, (16, ROWS), 0)
    for group in range(4):
        query_pos = query_pos + jnp.where(lane // 128 == group, ints[AT_QUERY + group], 0)
    for i in range(128):
        bias[i * 16 : i * 16 + 16, :] = jnp.where(ints[i] <= query_pos, 0.0, -jnp.inf)


def body(ints, *refs):
    pieces, (q_hbm, g_hbm, far_hbm, w_hbm) = refs[:8], refs[8:12]
    out_hbm, dq_hbm, far_out_hbm, wg_keep_hbm, wg_send_hbm, keep_hbm, send_hbm = refs[12:19]
    lat, q, g, far, w, lat_t, bias, keys, vals, scores, exps, dscores, dkv, rope = refs[19:33]
    out_b, dq_b, far_out, wg_b, keep, send, sems = refs[33:]
    used = []

    def copy(source, target):
        handle = pltpu.make_async_copy(source, target, sems.at[len(used)])
        used.append(handle)
        handle.start()
        return handle

    y_lo = ints[AT_YLO]
    loads = [copy(w_hbm.at[:, pl.ds(pl.multiple_of(y_lo * 1024, 1024), 1024)], w)]
    loads += [copy(piece, lat.at[pl.ds(i * 256, 256), :]) for i, piece in enumerate(pieces)]
    loads += [
        copy(q_hbm.at[:, pl.ds(pl.multiple_of(y_lo * 768, 256), 768)], q),
        copy(g_hbm.at[:, pl.ds(pl.multiple_of(y_lo * 512, 512), 512)], g),
        copy(far_hbm, far),
    ]
    for load in loads:
        load.wait()
    prepare(ints, lat, lat_t, bias, keys)

    chunks = [pl.ds(c * CHUNK, CHUNK) for c in range(KEYS // CHUNK)]
    q_t = jnp.concatenate([q[...].T, far[:, : 4 * QK].T], axis=1)
    g_t = jnp.concatenate([g[...].T, far[:, 4 * QK :].T], axis=1)
    q_h = [q_t[hh * QK : hh * QK + QK] for hh in range(4)]
    g_h = [g_t[hh * VDIM : hh * VDIM + VDIM] for hh in range(4)]
    top, norm, out, inverse, delta, q_s, g_s, dq = ([None] * 4 for _ in range(8))

    def project(pair, r):
        kv = mm(lat[r, :KV_RANK], w[:, pair * 512 : pair * 512 + 512]).astype(BF)
        for hh in range(2):
            keys[pair * 2 + hh, r, :NOPE] = kv[:, hh * 256 : hh * 256 + NOPE]
            vals[pair * 2 + hh, r, :] = kv[:, hh * 256 + NOPE : hh * 256 + 256]

    def score(hh, r):
        s = mm(keys[hh, r, :], q_h[hh]) + bias[r, :]
        scores[hh % 2, r, :] = s
        high = jnp.max(s.reshape(CHUNK // 8, 8, ROWS), axis=0)
        top[hh] = high if top[hh] is None else jnp.maximum(top[hh], high)

    def close_score(hh):
        top[hh] = jnp.max(top[hh], axis=0, keepdims=True) * SCALE_LOG2

    def weigh(hh, r):
        e = jnp.exp2(scores[hh % 2, r, :] * SCALE_LOG2 - top[hh])
        low = e.astype(BF)
        exps[hh % 2, r, :] = low
        total = jnp.sum(e.reshape(CHUNK // 8, 8, ROWS), axis=0)
        norm[hh] = total if norm[hh] is None else norm[hh] + total
        o_t = mm_first(vals[hh, r, :], low)
        out[hh] = o_t if out[hh] is None else out[hh] + o_t

    def close_weigh(hh):
        inv = 1.0 / jnp.sum(norm[hh], axis=0, keepdims=True)
        out[hh] = out[hh] * inv
        delta[hh] = jnp.sum(out[hh] * g_h[hh].astype(F32), axis=0, keepdims=True)
        inverse[hh] = inv
        q_s[hh] = (q_h[hh].astype(F32) * (inv * SCALE)).astype(BF)
        g_s[hh] = (g_h[hh].astype(F32) * inv).astype(BF)

    def back(hh, r):
        e = exps[hh % 2, r, :]
        dp = mm(vals[hh, r, :], g_h[hh])
        ds = (e.astype(F32) * (dp - delta[hh])).astype(BF)
        dscores[hh % 2, r, :] = ds
        dk = mm_last(ds, q_s[hh])
        dv = mm_last(e, g_s[hh])
        dkv[r, hh * 256 : hh * 256 + NOPE] = dk[:, :NOPE].astype(BF)
        dkv[r, hh * 256 + NOPE : hh * 256 + 256] = dv.astype(BF)
        if hh == 0:
            rope[r, :] = dk[:, NOPE:]
        else:
            rope[r, :] += dk[:, NOPE:]

    def query_grad(hh):
        dq[hh] = mm_first(keys[hh], dscores[hh % 2]) * (inverse[hh] * SCALE)

    def finish(pair):
        columns = slice(pair * 256, pair * 256 + 256)
        value = jnp.concatenate(out[pair * 2 : pair * 2 + 2], axis=0).T.astype(BF)
        out_b[:, columns] = value[:256]
        far_out[:, 768 + pair * 256 : 1024 + pair * 256] = value[256:]
        copy(out_b.at[:, columns], out_hbm.at[:, columns])
        columns = slice(pair * 384, pair * 384 + 384)
        value = jnp.concatenate(dq[pair * 2 : pair * 2 + 2], axis=0).T.astype(BF)
        dq_b[:, columns] = value[:256]
        far_out[:, columns] = value[256:]
        copy(dq_b.at[:, columns], dq_hbm.at[:, columns])
        columns = slice(pair * 512, pair * 512 + 512)
        wg = mm(lat_t[...], dkv[:, columns]).astype(BF)
        for k, target in enumerate((wg_keep_hbm, wg_send_hbm)):
            wg_b[k, :, columns] = wg[k * 256 : k * 256 + 256]
            copy(wg_b.at[k, :, columns], target.at[:, columns])

    def latent_terms(c):
        terms = mm_last(dkv[chunks[c], :], w[...]).astype(BF)
        tail = rope[chunks[c], :].astype(BF)
        for i in range(CHUNK // 32):
            block = c * (CHUNK // 32) + i
            index, target = ints[AT_TERM + block], keep if block < 32 else send
            target[index, :, :KV_RANK] = terms[i * 32 : i * 32 + 32]
            target[index, :, KV_RANK:] = tail[i * 32 : i * 32 + 32]

    for r in chunks:
        project(0, r)
        score(0, r)
    close_score(0)
    for r in chunks:
        score(1, r)
        weigh(0, r)
    close_score(1)
    close_weigh(0)
    for r in chunks:
        back(0, r)
        weigh(1, r)
    close_weigh(1)
    for r in chunks:
        back(1, r)
        project(1, r)
        score(2, r)
    close_score(2)
    query_grad(0)
    for r in chunks:
        score(3, r)
        weigh(2, r)
    close_score(3)
    close_weigh(2)
    query_grad(1)
    finish(0)
    for r in chunks:
        back(2, r)
        weigh(3, r)
    close_weigh(3)
    query_grad(2)
    order = list(range(len(chunks)))
    order = order[len(order) // 2 :] + order[: len(order) // 2]
    for c in order:
        back(3, chunks[c])
        latent_terms(c)
        if c == len(chunks) - 1:
            copy(send, send_hbm)
    copy(keep, keep_hbm)
    query_grad(3)
    finish(1)
    copy(far_out, far_out_hbm)
    for store in used[len(loads) :]:
        store.wait()


def attention(ints, pieces, queries, out_grad, far, up_weight):
    def shape(*dims):
        return jax.ShapeDtypeStruct(dims, BF)

    anywhere = pl.BlockSpec(memory_space=pl.ANY)
    return pl.pallas_call(
        body,
        in_specs=[pl.BlockSpec(memory_space=pltpu.SMEM)] + [anywhere] * 12,
        out_specs=[anywhere] * 7,
        out_shape=[
            shape(256, 4 * VDIM),
            shape(256, 4 * QK),
            shape(256, 4 * (QK + VDIM)),
            shape(256, 1024),
            shape(256, 1024),
            shape(32, 32, LAT),
            shape(32, 32, LAT),
        ],
        scratch_shapes=[
            pltpu.VMEM((KEYS, LAT), BF),
            pltpu.VMEM((256, 4 * QK), BF),
            pltpu.VMEM((256, 4 * VDIM), BF),
            pltpu.VMEM((256, 4 * (QK + VDIM)), BF),
            pltpu.VMEM((KV_RANK, 1024), BF),
            pltpu.VMEM((KV_RANK, KEYS), BF),
            pltpu.VMEM((KEYS, ROWS), F32),
            pltpu.VMEM((4, KEYS, QK), BF),
            pltpu.VMEM((4, KEYS, VDIM), BF),
            pltpu.VMEM((2, KEYS, ROWS), F32),
            pltpu.VMEM((2, KEYS, ROWS), BF),
            pltpu.VMEM((2, KEYS, ROWS), BF),
            pltpu.VMEM((KEYS, 1024), BF),
            pltpu.VMEM((KEYS, QK - NOPE), F32),
            pltpu.VMEM((256, 4 * VDIM), BF),
            pltpu.VMEM((256, 4 * QK), BF),
            pltpu.VMEM((256, 4 * (QK + VDIM)), BF),
            pltpu.VMEM((2, 256, 1024), BF),
            pltpu.VMEM((32, 32, LAT), BF),
            pltpu.VMEM((32, 32, LAT), BF),
            pltpu.SemaphoreType.DMA((32,)),
        ],
        compiler_params=pltpu.CompilerParams(vmem_limit_bytes=53 * 2**20),
        cost_estimate=pl.CostEstimate(
            flops=20 * 10**9, bytes_accessed=16 * 2**20, transcendentals=2**22
        ),
    )(ints, *pieces, queries, out_grad, far, up_weight)


AXES = ("ctx", "head")


def device_index(x, y, z, core):
    return ((y % 2) * 4 + x) * 16 + z * 4 + (y // 2) * 2 + core


def trade(value, first, second):
    pairs = []
    for x in range(4):
        for y in range(4):
            for z in range(4):
                for core, (a, b, c) in enumerate((first, second)):
                    pairs.append((device_index(x, y, z, core), device_index(x ^ a, y ^ b, z ^ c, core)))
    return lax.ppermute(value, AXES, pairs)


def swap_cores(value):
    return lax.ppermute(value, "head", [(i, i ^ 1) for i in range(16)])


def swap_ylo(value):
    return trade(value, (0, 1, 0), (0, 1, 0))


def shift(value, first, second):
    pairs = []
    for x in range(4):
        for y in range(4):
            for z in range(4):
                for core, (a, c) in enumerate((first, second)):
                    target = device_index((x + a) % 4, y, (z + c) % 4, core)
                    pairs.append((device_index(x, y, z, core), target))
    return lax.ppermute(value, AXES, pairs)


def exchange_rest(value):
    groups = [
        [device_index(x, yh * 2 + yl, z, 0) for z in range(4) for yl in range(2) for yh in range(2)]
        for x in range(4)
    ] + [
        [device_index(x, yh * 2 + yl, z, 1) for x in range(4) for yl in range(2) for yh in range(2)]
        for z in range(4)
    ]
    return lax.all_to_all(value, AXES, 0, 0, tiled=True, axis_index_groups=groups)


def gather_latent(latent, core):
    blocks = latent.reshape(4, 2, 2, 16, LAT)
    own = jnp.where(core == 0, blocks[:, :, 0], blocks[:, :, 1])
    pair = jnp.stack([own, swap_ylo(own)], axis=0)
    far = {k: shift(pair, (-k, 0), (-k, 0)) for k in (1, 3, 2)}
    mine = [pair, far[1], far[2], far[3]]
    return [piece.reshape(256, LAT) for piece in mine + [swap_cores(piece) for piece in mine]]


def kernel_ints(x, y_lo, z, core, group_order):
    def key_blocks(rel):
        return (x + rel // 2) % 4, y_lo ^ (rel % 2)

    block = jnp.arange(128, dtype=jnp.int32)
    which = core ^ (block // 64)
    far_x, far_y = key_blocks(block // 8 % 8)
    row = ((far_y * 4 + far_x) * 16 + block // 2 % 4 * 4 + block % 2 * 2 + which) * 16
    query = jnp.arange(4, dtype=jnp.int32)
    query = ((y_lo ^ (query // 2)) * 4 + x) * 2 + query % 2
    groups = jnp.concatenate([row // 128, query])
    onehot = groups[:, None] == jnp.arange(16, dtype=jnp.int32)[None, :]
    starts = jnp.sum(jnp.where(onehot, group_order[None, :], 0), axis=1) * 128
    starts = starts + jnp.concatenate([row % 128, jnp.zeros((4,), jnp.int32)])
    block = jnp.arange(8, dtype=jnp.int32)
    gap = (block % 4) ^ x
    slot = jnp.where(core == 0, (gap ^ gap // 2) % 2 * 2 + gap // 2, gap ^ (gap // 2))
    weight_rows = slot * 128 + ((block // 4) ^ y_lo) * 64
    block = jnp.arange(64, dtype=jnp.int32)
    far_x, far_y = key_blocks(block // 4 % 8)
    far_z = block % 4
    x_first = block // 8 % 4 * 8 + far_z * 2 + far_y
    z_first = (far_z - z + 4) % 4 * 8 + far_x * 2 + far_y
    terms = jnp.where((core ^ (block // 32)) == 0, x_first, z_first)
    return jnp.concatenate([starts, weight_rows, terms, y_lo[None]])


def sum_terms(first, others):
    total = first.astype(F32)
    for other in others:
        total = total + other.astype(F32)
    return total


def halves(y_lo, near, far, axis=1):
    low, high = jnp.where(y_lo == 0, near, far), jnp.where(y_lo == 0, far, near)
    return jnp.concatenate([low, high], axis=axis)


def other_half(y_lo, value):
    width = value.shape[1] // 2
    return jnp.where(y_lo == 0, value[:, width:], value[:, :width])


def reduce_terms(y_lo, out, dq, far_out, wg_keep, wg_send, keep, send):
    swapped = swap_cores(send)
    far_out = swap_ylo(far_out)
    wg_near = trade(wg_send, (1, 0, 0), (3, 0, 0))
    wire = [sum_terms(keep[8 * k : 8 * k + 8], [swapped[8 * k : 8 * k + 8]]) for k in range(4)]
    terms = [shift(wire[k].astype(BF), (k, 0), (0, k)) for k in (2, 1, 3)]
    wg_near = lax.optimization_barrier((wg_near, terms[0]))[0]
    wg_sum = sum_terms(wg_keep, [wg_near]).reshape(2, 2, 64, 1024)
    wire_wg = wg_sum.astype(BF)
    wg_terms = (
        trade(wire_wg[1, 0], (3, 0, 0), (1, 0, 0)),
        trade(wire_wg[1, 1], (3, 1, 0), (1, 1, 0)),
        swap_ylo(wire_wg[0, 1]),
    )
    part = sum_terms(wire[0], terms).astype(BF)
    far_out, wg_x, wg_xy, wg_y = lax.optimization_barrier((part, far_out, *wg_terms))[1:]
    moved = exchange_rest(part.reshape(16, 16, LAT))
    wg = halves(y_lo, sum_terms(wg_sum[0, 0], [wg_x]), sum_terms(wg_y, [wg_xy]))
    query_grad = halves(y_lo, dq, far_out[:, : 4 * QK])
    attn_output = halves(y_lo, out, far_out[:, 4 * QK :])
    latent_grad = sum_terms(moved[0], [moved[i] for i in range(1, 16)])
    return attn_output, query_grad, latent_grad, wg


def local(
    latent, queries, up_weight, out_grad, logratio, student_logprob, teacher_logprob, group_order
):
    ctx, head = lax.axis_index("ctx"), lax.axis_index("head")
    x, y_lo, z, core = ctx % 4, ctx // 4, head // 4, head % 2
    tok_weight = jnp.clip(jnp.exp(logratio), 0.8, 1.25) * (teacher_logprob - student_logprob)
    dout = (tok_weight[:, None] * out_grad.astype(F32)).astype(BF)
    far = jnp.concatenate([other_half(y_lo, queries), other_half(y_lo, dout)], axis=1)
    far = swap_ylo(far)
    pieces = gather_latent(latent, core)
    ints = kernel_ints(x, y_lo, z, core, group_order)
    results = attention(ints, pieces, queries, dout, far, up_weight)
    return reduce_terms(y_lo, *results)


def solution(mesh):
    placed = (
        P("ctx", None),
        P("ctx", "head"),
        P(None, "head"),
        P("ctx", "head"),
        P("ctx"),
        P("ctx"),
        P("ctx"),
        P(),
    )
    return jax.shard_map(
        local,
        mesh=mesh,
        in_specs=placed,
        out_specs=(P("ctx", "head"), P("ctx", "head"), P(AXES, None), P("ctx", "head")),
        check_vma=False,
    )
```

```python
import math

import jax
import jax.numpy as jnp
from jax import lax
from jax.experimental import pallas as pl
from jax.experimental.pallas import tpu as pltpu
from jax.sharding import PartitionSpec as P

NOPE = 128
VDIM = 128
KV_RANK = 512
QK = 192
LAT = 576
KEYS = 2048
ROWS = 512
CHUNK = 512
BF = jnp.bfloat16
F32 = jnp.float32
SCALE = QK ** -0.5
SCALE_LOG2 = SCALE * math.log2(math.e)
AT_QUERY, AT_WEIGHT, AT_TERM, AT_YLO = 128, 132, 140, 204


def mm(a, b):
    return jnp.dot(a, b, preferred_element_type=F32)


def mm_last(a, b):
    return lax.dot_general(a, b, (((1,), (1,)), ((), ())), preferred_element_type=F32)


def mm_first(a, b):
    return lax.dot_general(a, b, (((0,), (0,)), ((), ())), preferred_element_type=F32)


def prepare(ints, pieces, lat_t, bias, keys):
    for i, piece in enumerate(pieces):
        rows = slice(i * 256, i * 256 + 256)
        for hh in range(4):
            keys[hh, rows, NOPE:] = piece[:, KV_RANK:]
        for block in range(8):
            start = pl.multiple_of(ints[AT_WEIGHT + block], 64)
            lat_t[pl.ds(start, 64), rows] = piece[:, block * 64 : block * 64 + 64].T
    lane = lax.broadcasted_iota(jnp.int32, (16, ROWS), 1)
    query_pos = lane % 128 - lax.broadcasted_iota(jnp.int32, (16, ROWS), 0)
    for group in range(4):
        query_pos = query_pos + jnp.where(lane // 128 == group, ints[AT_QUERY + group], 0)
    for i in range(128):
        bias[i * 16 : i * 16 + 16, :] = jnp.where(ints[i] <= query_pos, 0.0, -jnp.inf)


def body(ints, *refs):
    pieces, (q_hbm, g_hbm, far, w_hbm) = refs[:8], refs[8:12]
    out_b, dq_b, far_out, wg_keep, wg_send, keep, send = refs[12:19]
    q, g, w, lat_t, bias, keys, vals, scores, exps, dscores, dkv, rope, sems = refs[19:]
    used = []

    def copy(source, target):
        handle = pltpu.make_async_copy(source, target, sems.at[len(used)])
        used.append(handle)
        handle.start()
        return handle

    y_lo = ints[AT_YLO]
    loads = [copy(w_hbm.at[:, pl.ds(pl.multiple_of(y_lo * 1024, 1024), 1024)], w)]
    loads += [
        copy(q_hbm.at[:, pl.ds(pl.multiple_of(y_lo * 768, 256), 768)], q),
        copy(g_hbm.at[:, pl.ds(pl.multiple_of(y_lo * 512, 512), 512)], g),
    ]
    for load in loads:
        load.wait()
    prepare(ints, pieces, lat_t, bias, keys)

    chunks = [pl.ds(c * CHUNK, CHUNK) for c in range(KEYS // CHUNK)]
    q_t = jnp.concatenate([q[...].T, far[:, : 4 * QK].T], axis=1)
    g_t = jnp.concatenate([g[...].T, far[:, 4 * QK :].T], axis=1)
    q_h = [q_t[hh * QK : hh * QK + QK] for hh in range(4)]
    g_h = [g_t[hh * VDIM : hh * VDIM + VDIM] for hh in range(4)]
    top, norm, out, inverse, delta, q_s, g_s, dq = ([None] * 4 for _ in range(8))

    def project(pair, r):
        first = r.start // 256
        lat = [piece[:, :KV_RANK] for piece in pieces[first : first + CHUNK // 256]]
        kv = mm(jnp.concatenate(lat, axis=0), w[:, pair * 512 : pair * 512 + 512]).astype(BF)
        for hh in range(2):
            keys[pair * 2 + hh, r, :NOPE] = kv[:, hh * 256 : hh * 256 + NOPE]
            vals[pair * 2 + hh, r, :] = kv[:, hh * 256 + NOPE : hh * 256 + 256]

    def score(hh, r):
        s = mm(keys[hh, r, :], q_h[hh]) + bias[r, :]
        scores[hh % 2, r, :] = s
        high = jnp.max(s.reshape(CHUNK // 8, 8, ROWS), axis=0)
        top[hh] = high if top[hh] is None else jnp.maximum(top[hh], high)

    def close_score(hh):
        top[hh] = jnp.max(top[hh], axis=0, keepdims=True) * SCALE_LOG2

    def weigh(hh, r):
        e = jnp.exp2(scores[hh % 2, r, :] * SCALE_LOG2 - top[hh])
        low = e.astype(BF)
        exps[hh % 2, r, :] = low
        total = jnp.sum(e.reshape(CHUNK // 8, 8, ROWS), axis=0)
        norm[hh] = total if norm[hh] is None else norm[hh] + total
        o_t = mm_first(vals[hh, r, :], low)
        out[hh] = o_t if out[hh] is None else out[hh] + o_t

    def close_weigh(hh):
        inv = 1.0 / jnp.sum(norm[hh], axis=0, keepdims=True)
        out[hh] = out[hh] * inv
        delta[hh] = jnp.sum(out[hh] * g_h[hh].astype(F32), axis=0, keepdims=True)
        inverse[hh] = inv
        q_s[hh] = (q_h[hh].astype(F32) * (inv * SCALE)).astype(BF)
        g_s[hh] = (g_h[hh].astype(F32) * inv).astype(BF)

    def back(hh, r):
        e = exps[hh % 2, r, :]
        dp = mm(vals[hh, r, :], g_h[hh])
        ds = (e.astype(F32) * (dp - delta[hh])).astype(BF)
        dscores[hh % 2, r, :] = ds
        dk = mm_last(ds, q_s[hh])
        dv = mm_last(e, g_s[hh])
        dkv[r, hh * 256 : hh * 256 + NOPE] = dk[:, :NOPE].astype(BF)
        dkv[r, hh * 256 + NOPE : hh * 256 + 256] = dv.astype(BF)
        if hh == 0:
            rope[r, :] = dk[:, NOPE:]
        else:
            rope[r, :] += dk[:, NOPE:]

    def query_grad(hh):
        dq[hh] = mm_first(keys[hh], dscores[hh % 2]) * (inverse[hh] * SCALE)

    def finish(pair):
        columns = slice(pair * 256, pair * 256 + 256)
        value = jnp.concatenate(out[pair * 2 : pair * 2 + 2], axis=0).T.astype(BF)
        out_b[:, columns] = value[:256]
        far_out[:, 768 + pair * 256 : 1024 + pair * 256] = value[256:]
        columns = slice(pair * 384, pair * 384 + 384)
        value = jnp.concatenate(dq[pair * 2 : pair * 2 + 2], axis=0).T.astype(BF)
        dq_b[:, columns] = value[:256]
        far_out[:, columns] = value[256:]
        columns = slice(pair * 512, pair * 512 + 512)
        wg = mm(lat_t[...], dkv[:, columns]).astype(BF)
        wg_keep[:, columns] = wg[:256]
        wg_send[:, columns] = wg[256:]

    def latent_terms(c):
        terms = mm_last(dkv[chunks[c], :], w[...]).astype(BF)
        tail = rope[chunks[c], :].astype(BF)
        for i in range(CHUNK // 32):
            block = c * (CHUNK // 32) + i
            index, target = ints[AT_TERM + block], keep if block < 32 else send
            target[index, :, :KV_RANK] = terms[i * 32 : i * 32 + 32]
            target[index, :, KV_RANK:] = tail[i * 32 : i * 32 + 32]

    for r in chunks:
        project(0, r)
        score(0, r)
    close_score(0)
    for r in chunks:
        score(1, r)
        weigh(0, r)
    close_score(1)
    close_weigh(0)
    for r in chunks:
        back(0, r)
        weigh(1, r)
    close_weigh(1)
    for r in chunks:
        back(1, r)
        project(1, r)
        score(2, r)
    close_score(2)
    query_grad(0)
    for r in chunks:
        score(3, r)
        weigh(2, r)
    close_score(3)
    close_weigh(2)
    query_grad(1)
    finish(0)
    for r in chunks:
        back(2, r)
        weigh(3, r)
    close_weigh(3)
    query_grad(2)
    order = list(range(len(chunks)))
    order = order[len(order) // 2 :] + order[: len(order) // 2]
    for c in order:
        back(3, chunks[c])
        latent_terms(c)
    query_grad(3)
    finish(1)


def attention(ints, pieces, queries, out_grad, far, up_weight):
    def shape(*dims):
        return jax.ShapeDtypeStruct(dims, BF)

    anywhere = pl.BlockSpec(memory_space=pl.ANY)
    inside = pl.BlockSpec(memory_space=pltpu.VMEM)
    return pl.pallas_call(
        body,
        in_specs=[pl.BlockSpec(memory_space=pltpu.SMEM)]
        + [inside] * 8
        + [anywhere, anywhere, inside, anywhere],
        out_specs=[inside] * 7,
        out_shape=[
            shape(256, 4 * VDIM),
            shape(256, 4 * QK),
            shape(256, 4 * (QK + VDIM)),
            shape(256, 1024),
            shape(256, 1024),
            shape(32, 32, LAT),
            shape(32, 32, LAT),
        ],
        scratch_shapes=[
            pltpu.VMEM((256, 4 * QK), BF),
            pltpu.VMEM((256, 4 * VDIM), BF),
            pltpu.VMEM((KV_RANK, 1024), BF),
            pltpu.VMEM((KV_RANK, KEYS), BF),
            pltpu.VMEM((KEYS, ROWS), F32),
            pltpu.VMEM((4, KEYS, QK), BF),
            pltpu.VMEM((4, KEYS, VDIM), BF),
            pltpu.VMEM((2, KEYS, ROWS), F32),
            pltpu.VMEM((2, KEYS, ROWS), BF),
            pltpu.VMEM((2, KEYS, ROWS), BF),
            pltpu.VMEM((KEYS, 1024), BF),
            pltpu.VMEM((KEYS, QK - NOPE), F32),
            pltpu.SemaphoreType.DMA((3,)),
        ],
        compiler_params=pltpu.CompilerParams(vmem_limit_bytes=46 * 2**20),
        cost_estimate=pl.CostEstimate(
            flops=20 * 10**9, bytes_accessed=16 * 2**20, transcendentals=2**22
        ),
    )(ints, *pieces, queries, out_grad, far, up_weight)


AXES = ("ctx", "head")


def device_index(x, y, z, core):
    return ((y % 2) * 4 + x) * 16 + z * 4 + (y // 2) * 2 + core


def trade(value, first, second):
    pairs = []
    for x in range(4):
        for y in range(4):
            for z in range(4):
                for core, (a, b, c) in enumerate((first, second)):
                    pairs.append((device_index(x, y, z, core), device_index(x ^ a, y ^ b, z ^ c, core)))
    return lax.ppermute(value, AXES, pairs)


def swap_cores(value):
    return lax.ppermute(value, "head", [(i, i ^ 1) for i in range(16)])


def swap_ylo(value):
    return trade(value, (0, 1, 0), (0, 1, 0))


def shift(value, first, second):
    pairs = []
    for x in range(4):
        for y in range(4):
            for z in range(4):
                for core, (a, c) in enumerate((first, second)):
                    target = device_index((x + a) % 4, y, (z + c) % 4, core)
                    pairs.append((device_index(x, y, z, core), target))
    return lax.ppermute(value, AXES, pairs)


def exchange_rest(value):
    groups = [
        [device_index(x, yh * 2 + yl, z, 0) for z in range(4) for yl in range(2) for yh in range(2)]
        for x in range(4)
    ] + [
        [device_index(x, yh * 2 + yl, z, 1) for x in range(4) for yl in range(2) for yh in range(2)]
        for z in range(4)
    ]
    return lax.all_to_all(value, AXES, 0, 0, tiled=True, axis_index_groups=groups)


def gather_latent(latent, core):
    blocks = latent.reshape(4, 2, 2, 16, LAT)
    own = jnp.where(core == 0, blocks[:, :, 0], blocks[:, :, 1])
    pair = jnp.stack([own, swap_ylo(own)], axis=0)
    far = {k: shift(pair, (-k, 0), (-k, 0)) for k in (1, 3, 2)}
    mine = [pair, far[1], far[2], far[3]]
    return [piece.reshape(256, LAT) for piece in mine + [swap_cores(piece) for piece in mine]]


def kernel_ints(x, y_lo, z, core, group_order):
    def key_blocks(rel):
        return (x + rel // 2) % 4, y_lo ^ (rel % 2)

    block = jnp.arange(128, dtype=jnp.int32)
    which = core ^ (block // 64)
    far_x, far_y = key_blocks(block // 8 % 8)
    row = ((far_y * 4 + far_x) * 16 + block // 2 % 4 * 4 + block % 2 * 2 + which) * 16
    query = jnp.arange(4, dtype=jnp.int32)
    query = ((y_lo ^ (query // 2)) * 4 + x) * 2 + query % 2
    groups = jnp.concatenate([row // 128, query])
    onehot = groups[:, None] == jnp.arange(16, dtype=jnp.int32)[None, :]
    starts = jnp.sum(jnp.where(onehot, group_order[None, :], 0), axis=1) * 128
    starts = starts + jnp.concatenate([row % 128, jnp.zeros((4,), jnp.int32)])
    block = jnp.arange(8, dtype=jnp.int32)
    gap = (block % 4) ^ x
    slot = jnp.where(core == 0, (gap ^ gap // 2) % 2 * 2 + gap // 2, gap ^ (gap // 2))
    weight_rows = slot * 128 + ((block // 4) ^ y_lo) * 64
    block = jnp.arange(64, dtype=jnp.int32)
    far_x, far_y = key_blocks(block // 4 % 8)
    far_z = block % 4
    x_first = block // 8 % 4 * 8 + far_z * 2 + far_y
    z_first = (far_z - z + 4) % 4 * 8 + far_x * 2 + far_y
    terms = jnp.where((core ^ (block // 32)) == 0, x_first, z_first)
    return jnp.concatenate([starts, weight_rows, terms, y_lo[None]])


def sum_terms(first, others):
    total = first.astype(F32)
    for other in others:
        total = total + other.astype(F32)
    return total


def halves(y_lo, near, far, axis=1):
    low, high = jnp.where(y_lo == 0, near, far), jnp.where(y_lo == 0, far, near)
    return jnp.concatenate([low, high], axis=axis)


def other_half(y_lo, value):
    width = value.shape[1] // 2
    return jnp.where(y_lo == 0, value[:, width:], value[:, :width])


def reduce_terms(y_lo, out, dq, far_out, wg_keep, wg_send, keep, send):
    swapped = swap_cores(send)
    far_out = swap_ylo(far_out)
    wg_near = trade(wg_send, (1, 0, 0), (3, 0, 0))
    wire = [sum_terms(keep[8 * k : 8 * k + 8], [swapped[8 * k : 8 * k + 8]]) for k in range(4)]
    terms = [shift(wire[k].astype(BF), (k, 0), (0, k)) for k in (2, 1, 3)]
    wg_near = lax.optimization_barrier((wg_near, terms[0]))[0]
    wg_sum = sum_terms(wg_keep, [wg_near]).reshape(2, 2, 64, 1024)
    wire_wg = wg_sum.astype(BF)
    wg_terms = (
        trade(wire_wg[1, 0], (3, 0, 0), (1, 0, 0)),
        trade(wire_wg[1, 1], (3, 1, 0), (1, 1, 0)),
        swap_ylo(wire_wg[0, 1]),
    )
    part = sum_terms(wire[0], terms).astype(BF)
    far_out, wg_x, wg_xy, wg_y = lax.optimization_barrier((part, far_out, *wg_terms))[1:]
    moved = exchange_rest(part.reshape(16, 16, LAT))
    wg = halves(y_lo, sum_terms(wg_sum[0, 0], [wg_x]), sum_terms(wg_y, [wg_xy]))
    query_grad = halves(y_lo, dq, far_out[:, : 4 * QK])
    attn_output = halves(y_lo, out, far_out[:, 4 * QK :])
    latent_grad = sum_terms(moved[0], [moved[i] for i in range(1, 16)])
    return attn_output, query_grad, latent_grad, wg


def local(
    latent, queries, up_weight, out_grad, logratio, student_logprob, teacher_logprob, group_order
):
    ctx, head = lax.axis_index("ctx"), lax.axis_index("head")
    x, y_lo, z, core = ctx % 4, ctx // 4, head // 4, head % 2
    tok_weight = jnp.clip(jnp.exp(logratio), 0.8, 1.25) * (teacher_logprob - student_logprob)
    dout = (tok_weight[:, None] * out_grad.astype(F32)).astype(BF)
    far = jnp.concatenate([other_half(y_lo, queries), other_half(y_lo, dout)], axis=1)
    far = swap_ylo(far)
    pieces = gather_latent(latent, core)
    ints = kernel_ints(x, y_lo, z, core, group_order)
    results = attention(ints, pieces, queries, dout, far, up_weight)
    return reduce_terms(y_lo, *results)


def solution(mesh):
    placed = (
        P("ctx", None),
        P("ctx", "head"),
        P(None, "head"),
        P("ctx", "head"),
        P("ctx"),
        P("ctx"),
        P("ctx"),
        P(),
    )
    return jax.shard_map(
        local,
        mesh=mesh,
        in_specs=placed,
        out_specs=(P("ctx", "head"), P("ctx", "head"), P(AXES, None), P("ctx", "head")),
        check_vma=False,
    )
```

```python
import math

import jax
import jax.numpy as jnp
from jax import lax
from jax.experimental import pallas as pl
from jax.experimental.pallas import tpu as pltpu
from jax.sharding import PartitionSpec as P

NOPE = 128
VDIM = 128
KV_RANK = 512
QK = 192
LAT = 576
KEYS = 2048
ROWS = 512
CHUNK = 512
BF = jnp.bfloat16
F32 = jnp.float32
SCALE = QK ** -0.5
SCALE_LOG2 = SCALE * math.log2(math.e)
AT_QUERY, AT_WEIGHT, AT_TERM = 128, 132, 140


def mm(a, b):
    return jnp.dot(a, b, preferred_element_type=F32)


def mm_last(a, b):
    return lax.dot_general(a, b, (((1,), (1,)), ((), ())), preferred_element_type=F32)


def mm_first(a, b):
    return lax.dot_general(a, b, (((0,), (0,)), ((), ())), preferred_element_type=F32)


def prepare(ints, pieces, lat_t, bias, keys):
    for i, piece in enumerate(pieces):
        rows = slice(i * 256, i * 256 + 256)
        for hh in range(4):
            keys[hh, rows, NOPE:] = piece[:, KV_RANK:]
        for block in range(8):
            start = pl.multiple_of(ints[AT_WEIGHT + block], 64)
            lat_t[pl.ds(start, 64), rows] = piece[:, block * 64 : block * 64 + 64].T
    lane = lax.broadcasted_iota(jnp.int32, (16, ROWS), 1)
    query_pos = lane % 128 - lax.broadcasted_iota(jnp.int32, (16, ROWS), 0)
    for group in range(4):
        query_pos = query_pos + jnp.where(lane // 128 == group, ints[AT_QUERY + group], 0)
    for i in range(128):
        bias[i * 16 : i * 16 + 16, :] = jnp.where(ints[i] <= query_pos, 0.0, -jnp.inf)


def body(ints, *refs):
    pieces, (q, g, far, w) = refs[:8], refs[8:12]
    out_b, dq_b, far_out, wg_keep, wg_send, keep, send = refs[12:19]
    lat_t, bias, keys, vals, scores, exps, dscores, dkv, rope = refs[19:]
    prepare(ints, pieces, lat_t, bias, keys)

    chunks = [pl.ds(c * CHUNK, CHUNK) for c in range(KEYS // CHUNK)]
    q_t = jnp.concatenate([q[...].T, far[:, : 4 * QK].T], axis=1)
    g_t = jnp.concatenate([g[...].T, far[:, 4 * QK :].T], axis=1)
    q_h = [q_t[hh * QK : hh * QK + QK] for hh in range(4)]
    g_h = [g_t[hh * VDIM : hh * VDIM + VDIM] for hh in range(4)]
    top, norm, out, inverse, delta, q_s, g_s, dq = ([None] * 4 for _ in range(8))

    def project(pair, r):
        first = r.start // 256
        lat = [piece[:, :KV_RANK] for piece in pieces[first : first + CHUNK // 256]]
        kv = mm(jnp.concatenate(lat, axis=0), w[:, pair * 512 : pair * 512 + 512]).astype(BF)
        for hh in range(2):
            keys[pair * 2 + hh, r, :NOPE] = kv[:, hh * 256 : hh * 256 + NOPE]
            vals[pair * 2 + hh, r, :] = kv[:, hh * 256 + NOPE : hh * 256 + 256]

    def score(hh, r):
        s = mm(keys[hh, r, :], q_h[hh]) + bias[r, :]
        scores[hh % 2, r, :] = s
        high = jnp.max(s.reshape(CHUNK // 8, 8, ROWS), axis=0)
        top[hh] = high if top[hh] is None else jnp.maximum(top[hh], high)

    def close_score(hh):
        top[hh] = jnp.max(top[hh], axis=0, keepdims=True) * SCALE_LOG2

    def weigh(hh, r):
        e = jnp.exp2(scores[hh % 2, r, :] * SCALE_LOG2 - top[hh])
        low = e.astype(BF)
        exps[hh % 2, r, :] = low
        total = jnp.sum(e.reshape(CHUNK // 8, 8, ROWS), axis=0)
        norm[hh] = total if norm[hh] is None else norm[hh] + total
        o_t = mm_first(vals[hh, r, :], low)
        out[hh] = o_t if out[hh] is None else out[hh] + o_t

    def close_weigh(hh):
        inv = 1.0 / jnp.sum(norm[hh], axis=0, keepdims=True)
        out[hh] = out[hh] * inv
        delta[hh] = jnp.sum(out[hh] * g_h[hh].astype(F32), axis=0, keepdims=True)
        inverse[hh] = inv
        q_s[hh] = (q_h[hh].astype(F32) * (inv * SCALE)).astype(BF)
        g_s[hh] = (g_h[hh].astype(F32) * inv).astype(BF)

    def back(hh, r):
        e = exps[hh % 2, r, :]
        dp = mm(vals[hh, r, :], g_h[hh])
        ds = (e.astype(F32) * (dp - delta[hh])).astype(BF)
        dscores[hh % 2, r, :] = ds
        dk = mm_last(ds, q_s[hh])
        dv = mm_last(e, g_s[hh])
        dkv[r, hh * 256 : hh * 256 + NOPE] = dk[:, :NOPE].astype(BF)
        dkv[r, hh * 256 + NOPE : hh * 256 + 256] = dv.astype(BF)
        if hh == 0:
            rope[r, :] = dk[:, NOPE:]
        else:
            rope[r, :] += dk[:, NOPE:]

    def query_grad(hh):
        dq[hh] = mm_first(keys[hh], dscores[hh % 2]) * (inverse[hh] * SCALE)

    def finish(pair):
        columns = slice(pair * 256, pair * 256 + 256)
        value = jnp.concatenate(out[pair * 2 : pair * 2 + 2], axis=0).T.astype(BF)
        out_b[:, columns] = value[:256]
        far_out[:, 768 + pair * 256 : 1024 + pair * 256] = value[256:]
        columns = slice(pair * 384, pair * 384 + 384)
        value = jnp.concatenate(dq[pair * 2 : pair * 2 + 2], axis=0).T.astype(BF)
        dq_b[:, columns] = value[:256]
        far_out[:, columns] = value[256:]
        columns = slice(pair * 512, pair * 512 + 512)
        wg = mm(lat_t[...], dkv[:, columns]).astype(BF)
        wg_keep[:, columns] = wg[:256]
        wg_send[:, columns] = wg[256:]

    def latent_terms(c):
        terms = mm_last(dkv[chunks[c], :], w[...]).astype(BF)
        tail = rope[chunks[c], :].astype(BF)
        for i in range(CHUNK // 32):
            block = c * (CHUNK // 32) + i
            index, target = ints[AT_TERM + block], keep if block < 32 else send
            target[index, :, :KV_RANK] = terms[i * 32 : i * 32 + 32]
            target[index, :, KV_RANK:] = tail[i * 32 : i * 32 + 32]

    for r in chunks:
        project(0, r)
        score(0, r)
    close_score(0)
    for r in chunks:
        score(1, r)
        weigh(0, r)
    close_score(1)
    close_weigh(0)
    for r in chunks:
        back(0, r)
        weigh(1, r)
    close_weigh(1)
    for r in chunks:
        back(1, r)
        project(1, r)
        score(2, r)
    close_score(2)
    query_grad(0)
    for r in chunks:
        score(3, r)
        weigh(2, r)
    close_score(3)
    close_weigh(2)
    query_grad(1)
    finish(0)
    for r in chunks:
        back(2, r)
        weigh(3, r)
    close_weigh(3)
    query_grad(2)
    order = list(range(len(chunks)))
    order = order[len(order) // 2 :] + order[: len(order) // 2]
    for c in order:
        back(3, chunks[c])
        latent_terms(c)
    query_grad(3)
    finish(1)


def attention(ints, pieces, queries, out_grad, far, up_weight):
    def shape(*dims):
        return jax.ShapeDtypeStruct(dims, BF)

    inside = pl.BlockSpec(memory_space=pltpu.VMEM)
    return pl.pallas_call(
        body,
        in_specs=[pl.BlockSpec(memory_space=pltpu.SMEM)]
        + [inside] * 12,
        out_specs=[inside] * 7,
        out_shape=[
            shape(256, 4 * VDIM),
            shape(256, 4 * QK),
            shape(256, 4 * (QK + VDIM)),
            shape(256, 1024),
            shape(256, 1024),
            shape(32, 32, LAT),
            shape(32, 32, LAT),
        ],
        scratch_shapes=[
            pltpu.VMEM((KV_RANK, KEYS), BF),
            pltpu.VMEM((KEYS, ROWS), F32),
            pltpu.VMEM((4, KEYS, QK), BF),
            pltpu.VMEM((4, KEYS, VDIM), BF),
            pltpu.VMEM((2, KEYS, ROWS), F32),
            pltpu.VMEM((2, KEYS, ROWS), BF),
            pltpu.VMEM((2, KEYS, ROWS), BF),
            pltpu.VMEM((KEYS, 1024), BF),
            pltpu.VMEM((KEYS, QK - NOPE), F32),
        ],
        compiler_params=pltpu.CompilerParams(vmem_limit_bytes=41 * 2**20),
        cost_estimate=pl.CostEstimate(
            flops=20 * 10**9, bytes_accessed=16 * 2**20, transcendentals=2**22
        ),
    )(ints, *pieces, queries, out_grad, far, up_weight)


AXES = ("ctx", "head")


def device_index(x, y, z, core):
    return ((y % 2) * 4 + x) * 16 + z * 4 + (y // 2) * 2 + core


def trade(value, first, second):
    pairs = []
    for x in range(4):
        for y in range(4):
            for z in range(4):
                for core, (a, b, c) in enumerate((first, second)):
                    pairs.append((device_index(x, y, z, core), device_index(x ^ a, y ^ b, z ^ c, core)))
    return lax.ppermute(value, AXES, pairs)


def swap_cores(value):
    return lax.ppermute(value, "head", [(i, i ^ 1) for i in range(16)])


def swap_ylo(value):
    return trade(value, (0, 1, 0), (0, 1, 0))


def shift(value, first, second):
    pairs = []
    for x in range(4):
        for y in range(4):
            for z in range(4):
                for core, (a, c) in enumerate((first, second)):
                    target = device_index((x + a) % 4, y, (z + c) % 4, core)
                    pairs.append((device_index(x, y, z, core), target))
    return lax.ppermute(value, AXES, pairs)


def exchange_rest(value):
    groups = [
        [device_index(x, yh * 2 + yl, z, 0) for z in range(4) for yl in range(2) for yh in range(2)]
        for x in range(4)
    ] + [
        [device_index(x, yh * 2 + yl, z, 1) for x in range(4) for yl in range(2) for yh in range(2)]
        for z in range(4)
    ]
    return lax.all_to_all(value, AXES, 0, 0, tiled=True, axis_index_groups=groups)


def gather_latent(latent, core):
    blocks = latent.reshape(4, 2, 2, 16, LAT)
    own = jnp.where(core == 0, blocks[:, :, 0], blocks[:, :, 1])
    pair = jnp.stack([own, swap_ylo(own)], axis=0)
    far = {k: shift(pair, (-k, 0), (-k, 0)) for k in (1, 3, 2)}
    mine = [pair, far[1], far[2], far[3]]
    pieces = mine + [swap_cores(piece) for piece in mine]
    return pair, [piece.reshape(256, LAT) for piece in pieces]


def kernel_ints(x, y_lo, z, core, group_order):
    def key_blocks(rel):
        return (x + rel // 2) % 4, y_lo ^ (rel % 2)

    block = jnp.arange(128, dtype=jnp.int32)
    which = core ^ (block // 64)
    far_x, far_y = key_blocks(block // 8 % 8)
    row = ((far_y * 4 + far_x) * 16 + block // 2 % 4 * 4 + block % 2 * 2 + which) * 16
    query = jnp.arange(4, dtype=jnp.int32)
    query = ((y_lo ^ (query // 2)) * 4 + x) * 2 + query % 2
    groups = jnp.concatenate([row // 128, query])
    onehot = groups[:, None] == jnp.arange(16, dtype=jnp.int32)[None, :]
    starts = jnp.sum(jnp.where(onehot, group_order[None, :], 0), axis=1) * 128
    starts = starts + jnp.concatenate([row % 128, jnp.zeros((4,), jnp.int32)])
    block = jnp.arange(8, dtype=jnp.int32)
    gap = (block % 4) ^ x
    slot = jnp.where(core == 0, (gap ^ gap // 2) % 2 * 2 + gap // 2, gap ^ (gap // 2))
    weight_rows = slot * 128 + ((block // 4) ^ y_lo) * 64
    block = jnp.arange(64, dtype=jnp.int32)
    far_x, far_y = key_blocks(block // 4 % 8)
    far_z = block % 4
    x_first = block // 8 % 4 * 8 + far_z * 2 + far_y
    z_first = (far_z - z + 4) % 4 * 8 + far_x * 2 + far_y
    terms = jnp.where((core ^ (block // 32)) == 0, x_first, z_first)
    return jnp.concatenate([starts, weight_rows, terms])


def sum_terms(first, others):
    total = first.astype(F32)
    for other in others:
        total = total + other.astype(F32)
    return total


def halves(y_lo, near, far, axis=1):
    low, high = jnp.where(y_lo == 0, near, far), jnp.where(y_lo == 0, far, near)
    return jnp.concatenate([low, high], axis=axis)


def own_half(y_lo, value):
    width = value.shape[1] // 2
    return jnp.where(y_lo == 0, value[:, :width], value[:, width:])


def other_half(y_lo, value):
    return own_half(1 - y_lo, value)


def reduce_terms(y_lo, out, dq, far_out, wg_keep, wg_send, keep, send):
    swapped = swap_cores(send)
    far_out = swap_ylo(far_out)
    wg_near = trade(wg_send, (1, 0, 0), (3, 0, 0))
    wire = [sum_terms(keep[8 * k : 8 * k + 8], [swapped[8 * k : 8 * k + 8]]) for k in range(4)]
    terms = [shift(wire[k].astype(BF), (k, 0), (0, k)) for k in (2, 1, 3)]
    wg_near = lax.optimization_barrier((wg_near, terms[0]))[0]
    wg_sum = sum_terms(wg_keep, [wg_near]).reshape(2, 2, 64, 1024)
    wire_wg = wg_sum.astype(BF)
    wg_terms = (
        trade(wire_wg[1, 0], (3, 0, 0), (1, 0, 0)),
        trade(wire_wg[1, 1], (3, 1, 0), (1, 1, 0)),
        swap_ylo(wire_wg[0, 1]),
    )
    part = sum_terms(wire[0], terms).astype(BF)
    far_out, wg_x, wg_xy, wg_y = lax.optimization_barrier((part, far_out, *wg_terms))[1:]
    moved = exchange_rest(part.reshape(16, 16, LAT))
    wg = halves(y_lo, sum_terms(wg_sum[0, 0], [wg_x]), sum_terms(wg_y, [wg_xy]))
    query_grad = halves(y_lo, dq, far_out[:, : 4 * QK])
    attn_output = halves(y_lo, out, far_out[:, 4 * QK :])
    latent_grad = sum_terms(moved[0], [moved[i] for i in range(1, 16)])
    return attn_output, query_grad, latent_grad, wg


def local(
    latent, queries, up_weight, out_grad, logratio, student_logprob, teacher_logprob, group_order
):
    ctx, head = lax.axis_index("ctx"), lax.axis_index("head")
    x, y_lo, z, core = ctx % 4, ctx // 4, head // 4, head % 2
    tok_weight = jnp.clip(jnp.exp(logratio), 0.8, 1.25) * (teacher_logprob - student_logprob)
    dout = (tok_weight[:, None] * out_grad.astype(F32)).astype(BF)
    far = jnp.concatenate([other_half(y_lo, queries), other_half(y_lo, dout)], axis=1)
    far = swap_ylo(far)
    pair, pieces = gather_latent(latent, core)
    ints = kernel_ints(x, y_lo, z, core, group_order)
    own = lax.optimization_barrier((queries, dout, up_weight, pair))[:3]
    own = [own_half(y_lo, value) for value in own]
    results = attention(ints, pieces, own[0], own[1], far, own[2])
    return reduce_terms(y_lo, *results)


def solution(mesh):
    placed = (
        P("ctx", None),
        P("ctx", "head"),
        P(None, "head"),
        P("ctx", "head"),
        P("ctx"),
        P("ctx"),
        P("ctx"),
        P(),
    )
    return jax.shard_map(
        local,
        mesh=mesh,
        in_specs=placed,
        out_specs=(P("ctx", "head"), P("ctx", "head"), P(AXES, None), P("ctx", "head")),
        check_vma=False,
    )
```
